256 devices in a mesh: grp: 16 (over z, core), atm: 16 (over y, x).
Axes of the slice: x: 4, y: 4, z: 8, core: 2. Of those that a mesh axis runs over, the one named last changes fastest.
Arguments:
- atoms: float32 [2, 65536, 128], P(None, ('grp', 'atm')), may hold values from -6 to 6
- kinds: int32 [2, 65536], P(None, ('grp', 'atm')), may hold values from 0 to 3
- member: int32 [2, 65536], P(None, ('grp', 'atm')), may hold values from 0 to 7
- targets: float32 [2, 128], replicated, may hold values from -900 to 900
- weights: float32 [128, 128], replicated, may hold values from -0.5 to 0.5
- bias: float32 [128], replicated, may hold values from -0.5 to 0.5
- readout: float32 [4, 128], replicated, may hold values from -0.5 to 0.5
- covariance: float32 [16384, 16384], P('grp', 'atm'), as said below
Outputs:
- posterior: float32 [16384, 16384], P('grp', 'atm')
- weights_out: float32 [128, 128], replicated
The draws below stay inside these ranges and needn't reach their ends.
Inputs may be any that keep to these rules, and one draw needn't show every extreme that they name: `covariance`: symmetric and positive definite.
All inputs are finite; a program needn't handle non-finite values.
Results may differ from the reference program's by a relative error of at most 0.0007.
Values sent between devices are 32-bit elements; how exact they have to be, the bound alone decides.
No kernel may reach another device: no remote copies, remote signals or barrier semaphores. Data moves between devices by JAX's collectives and lax.ppermute only.
A program may use at most 64 MiB of HBM per device.

```python
import math
import jax
import jax.numpy as jnp
from jax import lax

FEATURES = 128
PARAMS = 16384
GROUP_LOCAL = 8
GROUPS = 128
GROUP_ATOMS = 4096
ATOMS = 65536
TYPES = 4
STEPS = 2
N_GRP = 16


def draw_covariance(key, part):
    key_couple = jax.random.fold_in(key, 11)
    key_diag = jax.random.fold_in(key, 12)
    uniform_raw = jax.random.uniform(key_couple, (PARAMS, PARAMS), jnp.float32, -1.0, 1.0)
    coupling = (uniform_raw + uniform_raw.T) * (0.3 / math.sqrt(PARAMS))
    diag_values = jnp.exp(jax.random.uniform(key_diag, (PARAMS,), jnp.float32, math.log(0.8), math.log(1.6)))
    position = jnp.arange(PARAMS)
    base = coupling.at[position, position].add(diag_values)
    return base


def plant(entries, own_key, least, largest):
    dims = entries.shape
    place = [jax.random.randint(jax.random.fold_in(own_key, axis), (), 0, dims[axis]) for axis in range(len(dims))]
    entries = entries.at[tuple(place)].set(least)
    longest = dims.index(max(dims))
    place[longest] = (place[longest] + 1) % dims[longest]
    return entries.at[tuple(place)].set(largest)


def block_scale(stream_key, extent, pieces, smallest, largest):
    def one(dim, parts):
        heights = jax.random.uniform(jax.random.fold_in(jax.random.fold_in(stream_key, 6), dim), (parts,), jnp.float32, smallest / len(pieces), largest / len(pieces))
        return jnp.repeat(jnp.exp(heights), extent[dim] // parts).reshape((-1,) + (1,) * (len(extent) - dim - 1))

    level = one(*pieces[0])
    for cut in pieces[1:]:
        level = level * one(*cut)
    return level


def normal_values(stream_key, dims, spread, most, shards=(), held_as=jnp.bfloat16):
    gain = block_scale(stream_key, dims, shards, -0.22, 0.18) if shards else 1.0
    result = jax.random.normal(stream_key, dims, jnp.float32) * spread * gain
    return jnp.minimum(jnp.maximum(result, -most), most).astype(held_as)


def setup_inputs(seed: int = 0) -> dict:
    keys = jax.random.split(jax.random.key(seed), 9)
    return {
        "atoms": normal_values(keys[0], (STEPS, ATOMS, FEATURES), 1.0, 6.0, ((1, 256),), jnp.float32),
        "kinds": plant(jax.random.randint(keys[1], (STEPS, ATOMS), 0, TYPES), jax.random.fold_in(keys[1], 1), 0, TYPES - 1).astype(jnp.int32),
        "member": plant(jax.random.randint(keys[2], (STEPS, ATOMS), 0, GROUP_LOCAL), jax.random.fold_in(keys[2], 1), 0, GROUP_LOCAL - 1).astype(jnp.int32),
        "targets": normal_values(keys[3], (STEPS, GROUPS), 150.0, 900.0, (), jnp.float32),
        "weights": normal_values(keys[4], (FEATURES, FEATURES), FEATURES ** -0.5, 0.5, (), jnp.float32),
        "bias": jnp.clip(jax.random.uniform(keys[5], (FEATURES,), jnp.float32, -0.5, 0.5), -0.5, 0.5),
        "readout": normal_values(keys[6], (TYPES, FEATURES), FEATURES ** -0.5, 0.5, (), jnp.float32),
        "covariance": draw_covariance(jax.random.fold_in(keys[8], 71), 0),
    }


forget_rate = 0.98

def local_terms(atoms, kinds, member, weights, bias, readout):
    precise = lax.Precision.HIGHEST
    preact = jnp.dot(atoms.astype(jnp.float32), weights.astype(jnp.float32), precision=precise, preferred_element_type=jnp.float32) + bias
    hidden = jnp.tanh(preact)
    type_hot = (kinds[:, None] == jnp.arange(readout.shape[0])[None, :]).astype(jnp.float32)
    vectors = jnp.dot(type_hot, readout, precision=precise)
    atom_energy = jnp.sum(hidden * vectors, axis=1)
    slope = (1.0 - hidden * hidden) * vectors
    group_hot = (member[:, None] == jnp.arange(GROUP_LOCAL)[None, :]).astype(jnp.float32)
    energies = jnp.dot(atom_energy, group_hot, precision=precise)
    masked = atoms[:, None, :] * group_hot[:, :, None]
    grads = jnp.einsum('agi,ac->gic', masked, slope, precision=precise)
    return (energies, grads.reshape(GROUP_LOCAL, FEATURES * FEATURES))

def reference(atoms, kinds, member, targets, weights, bias, readout, covariance):
    precise = lax.Precision.HIGHEST
    current = weights
    covar = covariance
    identity = jnp.eye(GROUPS, dtype=jnp.float32)
    for update_idx in range(STEPS):

        def block_terms(inputs, current=current):
            return local_terms(inputs[0], inputs[1], inputs[2], current, bias, readout)
        energies, grads = lax.map(block_terms, (atoms[update_idx].reshape(N_GRP, GROUP_ATOMS, FEATURES), kinds[update_idx].reshape(N_GRP, GROUP_ATOMS), member[update_idx].reshape(N_GRP, GROUP_ATOMS)))
        predicted = energies.reshape(GROUPS)
        jacobian = grads.reshape(GROUPS, PARAMS)
        mismatch = targets[update_idx] - predicted
        gains = jnp.dot(covar, jacobian.T, precision=precise)
        curvature = jnp.dot(jacobian, gains, precision=precise)
        innovation = 0.5 * (curvature + curvature.T) + forget_rate * identity
        factor = jnp.linalg.cholesky(innovation)
        inverse = jax.scipy.linalg.cho_solve((factor, True), identity)
        coefficient = jnp.dot(inverse, mismatch, precision=precise)
        change = jnp.dot(gains, coefficient, precision=precise)
        current = current + change.reshape(FEATURES, FEATURES)
        scaled = jnp.dot(gains, inverse, precision=precise)
        covar = (covar - jnp.dot(scaled, gains.T, precision=precise)) / forget_rate
    return (covar, current)
```

```python
import jax
import jax.numpy as jnp
from jax import lax
from jax.sharding import PartitionSpec as P

FEATURES = 128
GROUP_LOCAL = 8
STEPS = 2

forget_rate = 0.98
precise = lax.Precision.HIGHEST


def local_terms(atoms, kinds, member, weights, bias, readout):
    preact = jnp.dot(atoms, weights, precision=precise, preferred_element_type=jnp.float32) + bias
    hidden = jnp.tanh(preact)
    type_hot = (kinds[:, None] == jnp.arange(readout.shape[0])[None, :]).astype(jnp.float32)
    vectors = jnp.dot(type_hot, readout, precision=precise)
    atom_energy = jnp.sum(hidden * vectors, axis=1)
    slope = (1.0 - hidden * hidden) * vectors
    group_hot = (member[:, None] == jnp.arange(GROUP_LOCAL)[None, :]).astype(jnp.float32)
    energies = jnp.dot(atom_energy, group_hot, precision=precise)
    masked = atoms[:, None, :] * group_hot[:, :, None]
    grads = jnp.einsum("agi,ac->gic", masked, slope, precision=precise)
    return (energies, grads.reshape(GROUP_LOCAL, FEATURES * FEATURES))


def exchange(chunks, axis):
    return lax.all_to_all(chunks, axis, 0, 0, tiled=True)


def spread(x, axis):
    return exchange(jnp.broadcast_to(x[None], (lax.axis_size(axis),) + x.shape), axis)


def swap(x, rows, cols):
    pairs = [(i * cols + j, j * cols + i) for i in range(rows) for j in range(cols)]
    return lax.ppermute(x, ("grp", "atm"), pairs)


def body(atoms, kinds, member, targets, weights, bias, readout, covariance):
    rows, cols = lax.axis_size("grp"), lax.axis_size("atm")
    group_total = GROUP_LOCAL * rows
    width = covariance.shape[1]
    lanes = FEATURES
    identity = jnp.eye(group_total, dtype=jnp.float32)
    current = weights
    covar = covariance
    for step in range(STEPS):
        energies, grads = local_terms(atoms[step], kinds[step], member[step], current, bias, readout)
        parts = grads.reshape(GROUP_LOCAL, cols, width).transpose(1, 0, 2)
        extra = jnp.broadcast_to(energies[None, :, None], (cols, GROUP_LOCAL, lanes))
        chunk = exchange(jnp.concatenate([parts, extra], axis=2), "atm").sum(axis=0)
        stacked = lax.all_gather(chunk, "grp", axis=0, tiled=True)
        jac = stacked[:, :width]
        mismatch = targets[step] - stacked[:, width]
        terms = lax.dot_general(jac, covar, (((1,), (1,)), ((), ())), precision=precise)
        own = exchange(terms.reshape(cols, group_total // cols, width), "atm").sum(axis=0)
        row_gains = lax.all_gather(own, "atm", axis=0, tiled=True)
        other = swap(own, rows, cols)
        part = lax.dot_general(other, jac, (((1,), (1,)), ((), ())), precision=precise)
        part = spread(part, "atm").sum(axis=0)
        stacked = lax.all_gather(jnp.concatenate([other, part], axis=1), "grp", axis=0, tiled=True)
        col_gains = stacked[:, :width]
        curvature = stacked[:, width:]
        innovation = 0.5 * (curvature + curvature.T) + forget_rate * identity
        factor = jnp.linalg.cholesky(innovation)
        inverse = jax.scipy.linalg.cho_solve((factor, True), identity)
        coefficient = jnp.dot(inverse, mismatch, precision=precise)
        change = jnp.dot(coefficient[None, :], col_gains, precision=precise)
        change = spread(change.reshape(width // FEATURES, FEATURES), "atm")
        current = current + change.reshape(FEATURES, FEATURES)
        scaled = jnp.dot(inverse, col_gains, precision=precise)
        downdate = lax.dot_general(row_gains, scaled, (((0,), (0,)), ((), ())), precision=precise)
        covar = (covar - downdate) / forget_rate
    return (covar, current)


def solution(mesh):
    return jax.shard_map(
        body,
        mesh=mesh,
        in_specs=(
            P(None, ("grp", "atm"), None),
            P(None, ("grp", "atm")),
            P(None, ("grp", "atm")),
            P(),
            P(),
            P(),
            P(),
            P("grp", "atm"),
        ),
        out_specs=(P("grp", "atm"), P()),
        check_vma=False,
    )
```

```python
import jax
import jax.numpy as jnp
from jax import lax
from jax.experimental import pallas as pl
from jax.experimental.pallas import tpu as pltpu
from jax.sharding import PartitionSpec as P

FEATURES = 128
GROUP_LOCAL = 8
STEPS = 2
SUB = 8

forget_rate = 0.98
precise = lax.Precision.HIGHEST
three = lax.Precision.HIGH


def dot(a, b, contract, precision):
    return lax.dot_general(
        a, b, ((contract[0], contract[1]), ((), ())), precision=precision, preferred_element_type=jnp.float32
    )


def block_inverse(p):
    m = len(p)
    if m == 1:
        return [[1.0 / p[0][0]]]
    if m == 2:
        a, b, d = p[0][0], p[0][1], p[1][1]
        r = 1.0 / (a * d - b * b)
        return [[d * r, -b * r], [-b * r, a * r]]
    h = m // 2
    top = [[p[i][j] for j in range(h)] for i in range(h)]
    side = [[p[i][h + j] for j in range(h)] for i in range(h)]
    ti = block_inverse(top)
    ts = [[sum(ti[i][k] * side[k][j] for k in range(h)) for j in range(h)] for i in range(h)]
    schur = [[None] * h for _ in range(h)]
    for i in range(h):
        for j in range(i, h):
            schur[i][j] = p[h + i][h + j] - sum(side[k][i] * ts[k][j] for k in range(h))
            schur[j][i] = schur[i][j]
    si = block_inverse(schur)
    tss = [[sum(ts[i][k] * si[k][j] for k in range(h)) for j in range(h)] for i in range(h)]
    out = [[None] * m for _ in range(m)]
    for i in range(h):
        for j in range(h):
            out[i][h + j] = -tss[i][j]
            out[h + j][i] = -tss[i][j]
            out[h + i][h + j] = si[i][j]
            if j >= i:
                out[i][j] = ti[i][j] + sum(tss[i][k] * ts[j][k] for k in range(h))
                out[j][i] = out[i][j]
    return out


def sweep_inverse(tiles):
    n = tiles[0].shape[1]
    full = (SUB, n)
    lane = lax.broadcasted_iota(jnp.int32, full, 1)
    sub = lax.broadcasted_iota(jnp.int32, full, 0)
    for t in range(n // SUB):
        k = t * SUB
        inside = (lane >= k) & (lane < k + SUB)
        rows = [jnp.broadcast_to(tiles[t][u : u + 1, :], full) for u in range(SUB)]
        cols = [[jnp.broadcast_to(x[:, k + u : k + u + 1], full) for u in range(SUB)] for x in tiles]
        piv = [[None] * SUB for _ in range(SUB)]
        for u in range(SUB):
            for v in range(u, SUB):
                piv[u][v] = jnp.broadcast_to(cols[t][v][u : u + 1, :], full)
                piv[v][u] = piv[u][v]
        inv = block_inverse(piv)
        rows = [jnp.where(inside, (lane == k + u).astype(jnp.float32), rows[u]) for u in range(SUB)]
        w = [sum(inv[u][v] * rows[v] for v in range(SUB)) for u in range(SUB)]
        new = []
        for i, x in enumerate(tiles):
            if i == t:
                y = w[0]
                for u in range(1, SUB):
                    y = jnp.where(sub == u, w[u], y)
            else:
                y = jnp.where(inside, 0.0, x)
                for u in range(SUB):
                    y = y - cols[i][u] * w[u]
            new.append(y)
        tiles = new
    return tiles


def update_kernel(stacked_ref, mismatch_ref, inverse_ref, change_ref):
    n = mismatch_ref.shape[0]
    width = stacked_ref.shape[1] - n
    curvature = stacked_ref[:, width:]
    row = lax.broadcasted_iota(jnp.int32, (n, n), 0)
    col = lax.broadcasted_iota(jnp.int32, (n, n), 1)
    innovation = 0.5 * (curvature + curvature.T) + jnp.where(row == col, forget_rate, 0.0)
    tiles = sweep_inverse([innovation[SUB * i : SUB * i + SUB] for i in range(n // SUB)])
    total = jnp.zeros((SUB, n), jnp.float32)
    for i, x in enumerate(tiles):
        inverse_ref[SUB * i : SUB * i + SUB, :] = x
        total = total + x * mismatch_ref[SUB * i : SUB * i + SUB, :]
    coefficient = jnp.broadcast_to(jnp.sum(total, axis=0, keepdims=True), (SUB, n))
    moved = jnp.dot(coefficient, stacked_ref[:, :width], precision=precise, preferred_element_type=jnp.float32)
    sub = lax.broadcasted_iota(jnp.int32, (SUB, FEATURES), 0)
    change = moved[:, :FEATURES]
    for r in range(1, width // FEATURES):
        change = jnp.where(sub == r, moved[:, r * FEATURES : (r + 1) * FEATURES], change)
    for j in range(change_ref.shape[0]):
        change_ref[j] = change


def solve_update(stacked, mismatch, copies):
    n = mismatch.shape[0]
    vmem = pl.BlockSpec(memory_space=pltpu.VMEM)
    return pl.pallas_call(
        update_kernel,
        out_shape=(
            jax.ShapeDtypeStruct((n, n), jnp.float32),
            jax.ShapeDtypeStruct((copies, SUB, FEATURES), jnp.float32),
        ),
        in_specs=[vmem, vmem],
        out_specs=(vmem, vmem),
        name="inverse_and_change",
    )(stacked, mismatch)


def exchange(chunks, axis):
    return lax.all_to_all(chunks, axis, 0, 0, tiled=True)


def spread(x, axis):
    return exchange(jnp.broadcast_to(x[None], (lax.axis_size(axis),) + x.shape), axis)


def swap(x, rows, cols):
    pairs = [(i * cols + j, j * cols + i) for i in range(rows) for j in range(cols)]
    return lax.ppermute(x, ("grp", "atm"), pairs)


def gather_rows(own):
    twice = jnp.concatenate([own, own], axis=0)
    got = lax.all_gather(twice, "atm", axis=0, tiled=False)
    return got[:, : own.shape[0]].reshape(-1, own.shape[1])


def vectors_of(kinds, readout):
    type_hot = (kinds[:, None] == jnp.arange(readout.shape[0])[None, :]).astype(jnp.float32)
    return jnp.dot(type_hot, readout, precision=precise)


def group_hot_of(member):
    return (jnp.arange(GROUP_LOCAL)[:, None] == member[None, :]).astype(jnp.float32)


def layer(atoms, weights, bias, vectors):
    hidden = jnp.tanh(jnp.dot(atoms, weights, precision=precise, preferred_element_type=jnp.float32) + bias)
    return hidden * vectors, (1.0 - hidden * hidden) * vectors


def first_chunk(atoms, kinds, member, weights, bias, readout, cols, width):
    energy, slope = layer(atoms, weights, bias, vectors_of(kinds, readout))
    group_hot = group_hot_of(member)
    energies = jnp.sum(dot(group_hot, energy, ((1,), (0,)), precise), axis=1)
    masked = atoms[:, None, :] * group_hot.T[:, :, None]
    grads = jnp.einsum("agi,ac->gic", masked, slope, precision=precise)
    parts = grads.reshape(GROUP_LOCAL, cols, width).transpose(1, 0, 2)
    extra = jnp.broadcast_to(energies[None, :, None], (cols, GROUP_LOCAL, FEATURES))
    return exchange(jnp.concatenate([parts, extra], axis=2), "atm").sum(axis=0)


def gather_atoms(atoms, kinds, member):
    pad = jnp.zeros((4, FEATURES), jnp.float32)
    extra = [x.astype(jnp.float32).reshape(-1, FEATURES) for x in (kinds, member)]
    got = lax.all_gather(jnp.concatenate([atoms, *extra, pad], axis=0), "atm", axis=0, tiled=False)
    local = atoms.shape[0]
    lines = local // FEATURES
    kinds = got[:, local : local + lines].reshape(-1)
    member = got[:, local + lines : local + 2 * lines].reshape(-1)
    return got[:, :local].reshape(-1, FEATURES), kinds, member


def later_terms(gathered, readout, col_index, width):
    atoms, kinds, member = gathered
    group_hot = group_hot_of(member)
    count = width // FEATURES
    part = lax.dynamic_slice_in_dim(atoms, col_index * count, count, 1).T
    masked = (group_hot[:, None, :] * part[None, :, :]).reshape(GROUP_LOCAL * count, -1)
    return atoms, vectors_of(kinds, readout), group_hot, masked


def later_chunk(terms, weights, bias, width):
    atoms, vectors, group_hot, masked = terms
    energy, slope = layer(atoms, weights, bias, vectors)
    energies = jnp.sum(dot(group_hot, energy, ((1,), (0,)), precise), axis=1, keepdims=True)
    grads = dot(masked, slope, ((1,), (0,)), precise).reshape(GROUP_LOCAL, width)
    return jnp.concatenate([grads, jnp.broadcast_to(energies, (GROUP_LOCAL, FEATURES))], axis=1)


def together(*values):
    return lax.optimization_barrier(values)


def body(atoms, kinds, member, targets, weights, bias, readout, covariance):
    rows, cols = lax.axis_size("grp"), lax.axis_size("atm")
    col_index = lax.axis_index("atm")
    group_total = GROUP_LOCAL * rows
    width = covariance.shape[1]
    current = weights
    gathered = gather_atoms(atoms[1], kinds[1], member[1])
    row_gains, scaled = [], []
    for step in range(STEPS):
        if step == 0:
            chunk = first_chunk(atoms[0], kinds[0], member[0], current, bias, readout, cols, width)
        else:
            chunk = later_chunk(later, current, bias, width)
        stacked = lax.all_gather(chunk, "grp", axis=0, tiled=True)
        jac = stacked[:, :width]
        mismatch = targets[step][:, None] - stacked[:, width:]
        terms = dot(jac, covariance, ((1,), (1,)), three)
        for gains, part in zip(row_gains, scaled):
            terms = (terms - dot(dot(jac, part, ((1,), (1,)), precise), gains, ((1,), (0,)), precise)) / forget_rate
        own = exchange(terms.reshape(cols, group_total // cols, width), "atm").sum(axis=0)
        if step == 0:
            own, *gathered = together(own, *gathered)
            later = later_terms(gathered, readout, col_index, width)
        row_gains.append(gather_rows(own))
        other = swap(own, rows, cols)
        part = dot(other, jac, ((1,), (1,)), precise)
        part = spread(part, "atm").sum(axis=0)
        if step == 0:
            part, *later = together(part, *later)
        stacked = lax.all_gather(jnp.concatenate([other, part], axis=1), "grp", axis=0, tiled=True)
        inverse, change = solve_update(stacked, mismatch, cols)
        current = current + exchange(change, "atm").reshape(FEATURES, FEATURES)
        scaled.append(dot(inverse, stacked[:, :width], ((1,), (0,)), precise))
    left = jnp.concatenate(row_gains, axis=0)
    right = jnp.concatenate([x / forget_rate ** (STEPS - i) for i, x in enumerate(scaled)], axis=0)
    covar = covariance / forget_rate**STEPS - dot(left, right, ((0,), (0,)), three)
    return (covar, current)


def solution(mesh):
    return jax.shard_map(
        body,
        mesh=mesh,
        in_specs=(
            P(None, ("grp", "atm"), None),
            P(None, ("grp", "atm")),
            P(None, ("grp", "atm")),
            P(),
            P(),
            P(),
            P(),
            P("grp", "atm"),
        ),
        out_specs=(P("grp", "atm"), P()),
        check_vma=False,
    )
```

```python
import functools
import math

import jax
import jax.numpy as jnp
from jax import lax
from jax.experimental import pallas as pl
from jax.experimental.pallas import tpu as pltpu
from jax.sharding import PartitionSpec as P

FEATURES = 128
GROUP_LOCAL = 8
STEPS = 2
SUB = 8

forget_rate = 0.98
precise = lax.Precision.HIGHEST
three = lax.Precision.HIGH


def dot(a, b, contract, precision):
    return lax.dot_general(
        a, b, ((contract[0], contract[1]), ((), ())), precision=precision, preferred_element_type=jnp.float32
    )


def block_inverse(p):
    m = len(p)
    if m == 1:
        return [[1.0 / p[0][0]]]
    if m == 2:
        a, b, d = p[0][0], p[0][1], p[1][1]
        r = 1.0 / (a * d - b * b)
        return [[d * r, -b * r], [-b * r, a * r]]
    h = m // 2
    top = [[p[i][j] for j in range(h)] for i in range(h)]
    side = [[p[i][h + j] for j in range(h)] for i in range(h)]
    ti = block_inverse(top)
    ts = [[sum(ti[i][k] * side[k][j] for k in range(h)) for j in range(h)] for i in range(h)]
    schur = [[None] * h for _ in range(h)]
    for i in range(h):
        for j in range(i, h):
            schur[i][j] = p[h + i][h + j] - sum(side[k][i] * ts[k][j] for k in range(h))
            schur[j][i] = schur[i][j]
    si = block_inverse(schur)
    tss = [[sum(ts[i][k] * si[k][j] for k in range(h)) for j in range(h)] for i in range(h)]
    out = [[None] * m for _ in range(m)]
    for i in range(h):
        for j in range(h):
            out[i][h + j] = -tss[i][j]
            out[h + j][i] = -tss[i][j]
            out[h + i][h + j] = si[i][j]
            if j >= i:
                out[i][j] = ti[i][j] + sum(tss[i][k] * ts[j][k] for k in range(h))
                out[j][i] = out[i][j]
    return out


def total(values):
    values = list(values)
    while len(values) > 1:
        values = [values[i] + values[i + 1] if i + 1 < len(values) else values[i] for i in range(0, len(values), 2)]
    return values[0]


def sweep_inverse(tiles):
    n = tiles[0].shape[1]
    full = (SUB, n)
    lane = lax.broadcasted_iota(jnp.int32, (1, n), 1)
    sub = lax.broadcasted_iota(jnp.int32, (SUB, 1), 0)
    for t in range(n // SUB):
        k = t * SUB
        inside = (lane >= k) & (lane < k + SUB)
        rows = [tiles[t][u : u + 1, :] for u in range(SUB)]
        cols = [[jnp.broadcast_to(x[:, k + u : k + u + 1], full) for u in range(SUB)] for x in tiles]
        piv = [[cols[t][v][u : u + 1, :] for v in range(SUB)] for u in range(SUB)]
        inv = block_inverse(piv)
        rows = [jnp.where(inside, (lane == k + u).astype(jnp.float32), rows[u]) for u in range(SUB)]
        w = [total(inv[u][v] * rows[v] for v in range(SUB)) for u in range(SUB)]
        new = []
        for i, x in enumerate(tiles):
            if i == t:
                y = jnp.broadcast_to(w[0], full)
                for u in range(1, SUB):
                    y = jnp.where(sub == u, w[u], y)
            else:
                y = jnp.where(inside, 0.0, x) - total(cols[i][u] * w[u] for u in range(SUB))
            new.append(y)
        tiles = new
    return tiles


def update_kernel(order, stacked_ref, mismatch_ref, inverse_ref, change_ref):
    n = mismatch_ref.shape[0]
    width = stacked_ref.shape[1] - n
    places = [order.index(t) * SUB for t in range(n // SUB)]
    curvature = jnp.concatenate([stacked_ref[p : p + SUB, width:] for p in places], axis=0)
    row = lax.broadcasted_iota(jnp.int32, (n, n), 0)
    col = lax.broadcasted_iota(jnp.int32, (n, n), 1)
    innovation = 0.5 * (curvature + curvature.T) + jnp.where(row == col, forget_rate, 0.0)
    tiles = sweep_inverse([innovation[SUB * i : SUB * i + SUB] for i in range(n // SUB)])
    for p, x in zip(places, tiles):
        inverse_ref[p : p + SUB, :] = x
    weighted = total(x * mismatch_ref[SUB * i : SUB * i + SUB, :] for i, x in enumerate(tiles))
    coefficient = jnp.broadcast_to(jnp.sum(weighted, axis=0, keepdims=True), (SUB, n))
    gains = jnp.concatenate([stacked_ref[p : p + SUB, :width] for p in places], axis=0)
    moved = jnp.dot(coefficient, gains, precision=precise, preferred_element_type=jnp.float32)
    sub = lax.broadcasted_iota(jnp.int32, (SUB, FEATURES), 0)
    change = moved[:, :FEATURES]
    for r in range(1, width // FEATURES):
        change = jnp.where(sub == r, moved[:, r * FEATURES : (r + 1) * FEATURES], change)
    for j in range(change_ref.shape[0]):
        change_ref[j] = change


def solve_update(stacked, mismatch, copies, order):
    n = mismatch.shape[0]
    vmem = pl.BlockSpec(memory_space=pltpu.VMEM)
    return pl.pallas_call(
        functools.partial(update_kernel, order),
        out_shape=(
            jax.ShapeDtypeStruct((n, n), jnp.float32),
            jax.ShapeDtypeStruct((copies, SUB, FEATURES), jnp.float32),
        ),
        in_specs=[vmem, vmem],
        out_specs=(vmem, vmem),
        compiler_params=pltpu.CompilerParams(vmem_limit_bytes=8 * 1024 * 1024),
        name="inverse_and_change",
    )(stacked, mismatch)


def exchange(chunks, axis):
    return lax.all_to_all(chunks, axis, 0, 0, tiled=True)


def spread(x, axis):
    return exchange(jnp.broadcast_to(x[None], (lax.axis_size(axis),) + x.shape), axis)


def far_row(j, side):
    return (j // side + side // 2) % side * side + (j % side + side // 2) % side


def swap(x, order):
    size = len(order)
    pairs = [(i * size + order[a], a * size + i) for i in range(size) for a in range(size)]
    return lax.ppermute(x, ("grp", "atm"), pairs)


def gather_rows(own):
    twice = jnp.concatenate([own, own], axis=0)
    got = lax.all_gather(twice, "atm", axis=0, tiled=False)
    return got[:, : own.shape[0]].reshape(-1, own.shape[1])


def vectors_of(kinds, readout):
    type_hot = (kinds[:, None] == jnp.arange(readout.shape[0])[None, :]).astype(jnp.float32)
    return jnp.dot(type_hot, readout, precision=precise)


def group_hot_of(member):
    return (jnp.arange(GROUP_LOCAL)[:, None] == member[None, :]).astype(jnp.float32)


def layer(atoms, weights, bias, vectors):
    hidden = jnp.tanh(jnp.dot(atoms, weights, precision=precise, preferred_element_type=jnp.float32) + bias)
    return hidden * vectors, (1.0 - hidden * hidden) * vectors


def first_chunk(atoms, kinds, member, weights, bias, readout, cols, width):
    energy, slope = layer(atoms, weights, bias, vectors_of(kinds, readout))
    group_hot = group_hot_of(member)
    energies = jnp.sum(dot(group_hot, energy, ((1,), (0,)), precise), axis=1)
    masked = atoms[:, None, :] * group_hot.T[:, :, None]
    grads = jnp.einsum("agi,ac->gic", masked, slope, precision=precise)
    parts = grads.reshape(GROUP_LOCAL, cols, width).transpose(1, 0, 2)
    extra = jnp.broadcast_to(energies[None, :, None], (cols, GROUP_LOCAL, FEATURES))
    return exchange(jnp.concatenate([parts, extra], axis=2), "atm").sum(axis=0)


def gather_atoms(atoms, kinds, member):
    pad = jnp.zeros((4, FEATURES), jnp.float32)
    extra = [x.astype(jnp.float32).reshape(-1, FEATURES) for x in (kinds, member)]
    got = lax.all_gather(jnp.concatenate([atoms, *extra, pad], axis=0), "atm", axis=0, tiled=False)
    local = atoms.shape[0]
    lines = local // FEATURES
    kinds = got[:, local : local + lines].reshape(-1)
    member = got[:, local + lines : local + 2 * lines].reshape(-1)
    return got[:, :local].reshape(-1, FEATURES), kinds, member


def later_terms(gathered, readout, col_index, width):
    atoms, kinds, member = gathered
    group_hot = group_hot_of(member)
    count = width // FEATURES
    part = lax.dynamic_slice_in_dim(atoms, col_index * count, count, 1).T
    masked = (group_hot[:, None, :] * part[None, :, :]).reshape(GROUP_LOCAL * count, -1)
    return atoms, vectors_of(kinds, readout), group_hot, masked


def later_chunk(terms, weights, bias, width):
    atoms, vectors, group_hot, masked = terms
    energy, slope = layer(atoms, weights, bias, vectors)
    energies = jnp.sum(dot(group_hot, energy, ((1,), (0,)), precise), axis=1, keepdims=True)
    grads = dot(masked, slope, ((1,), (0,)), precise).reshape(GROUP_LOCAL, width)
    return jnp.concatenate([grads, jnp.broadcast_to(energies, (GROUP_LOCAL, FEATURES))], axis=1)


def together(*values):
    return lax.optimization_barrier(values)


def body(atoms, kinds, member, targets, weights, bias, readout, covariance):
    rows, cols = lax.axis_size("grp"), lax.axis_size("atm")
    col_index = lax.axis_index("atm")
    group_total = GROUP_LOCAL * rows
    width = covariance.shape[1]
    order = [far_row(a, math.isqrt(rows)) for a in range(rows)]
    current = weights
    gathered = gather_atoms(atoms[1], kinds[1], member[1])
    row_gains, scaled = [], []
    for step in range(STEPS):
        if step == 0:
            chunk = first_chunk(atoms[0], kinds[0], member[0], current, bias, readout, cols, width)
        else:
            chunk = later_chunk(later, current, bias, width)
        stacked = lax.all_gather(chunk, "grp", axis=0, tiled=True)
        jac = stacked[:, :width]
        mismatch = targets[step][:, None] - stacked[:, width:]
        terms = dot(jac, covariance, ((1,), (1,)), three)
        for gains, part in zip(row_gains, scaled):
            terms = (terms - dot(dot(jac, part, ((1,), (1,)), precise), gains, ((1,), (0,)), precise)) / forget_rate
        own = exchange(terms.reshape(cols, group_total // cols, width), "atm").sum(axis=0)
        if step == 0:
            own, *gathered = together(own, *gathered)
            later = later_terms(gathered, readout, col_index, width)
        row_gains.append(gather_rows(own))
        other = swap(own, order)
        part = dot(other, jac, ((1,), (1,)), precise)
        part = spread(part, "atm").sum(axis=0)
        if step == 0:
            part, *later = together(part, *later)
        stacked = lax.all_gather(jnp.concatenate([other, part], axis=1), "grp", axis=0, tiled=True)
        inverse, change = solve_update(stacked, mismatch, cols, order)
        if step == STEPS - 1:
            change, *row_gains = together(change, *row_gains)
        current = current + exchange(change, "atm").reshape(FEATURES, FEATURES)
        scaled.append(dot(inverse, stacked[:, :width], ((0,), (0,)), precise))
    left = jnp.concatenate(row_gains, axis=0)
    right = jnp.concatenate([x / forget_rate ** (STEPS - i) for i, x in enumerate(scaled)], axis=0)
    covar = covariance / forget_rate**STEPS - dot(left, right, ((0,), (0,)), three)
    return (covar, current)


def solution(mesh):
    return jax.shard_map(
        body,
        mesh=mesh,
        in_specs=(
            P(None, ("grp", "atm"), None),
            P(None, ("grp", "atm")),
            P(None, ("grp", "atm")),
            P(),
            P(),
            P(),
            P(),
            P("grp", "atm"),
        ),
        out_specs=(P("grp", "atm"), P()),
        check_vma=False,
    )
```

```python
import functools
import math

import jax
import jax.numpy as jnp
from jax import lax
from jax.experimental import pallas as pl
from jax.experimental.pallas import tpu as pltpu
from jax.sharding import PartitionSpec as P

FEATURES = 128
GROUP_LOCAL = 8
STEPS = 2
SUB = 8

forget_rate = 0.98
precise = lax.Precision.HIGHEST
three = lax.Precision.HIGH
MIB = 1024 * 1024


def dot(a, b, contract, precision):
    return lax.dot_general(
        a, b, ((contract[0], contract[1]), ((), ())), precision=precision, preferred_element_type=jnp.float32
    )


def block_inverse(p):
    m = len(p)
    if m == 1:
        return [[1.0 / p[0][0]]]
    if m == 2:
        a, b, d = p[0][0], p[0][1], p[1][1]
        r = 1.0 / (a * d - b * b)
        return [[d * r, -b * r], [-b * r, a * r]]
    h = m // 2
    top = [[p[i][j] for j in range(h)] for i in range(h)]
    side = [[p[i][h + j] for j in range(h)] for i in range(h)]
    ti = block_inverse(top)
    ts = [[sum(ti[i][k] * side[k][j] for k in range(h)) for j in range(h)] for i in range(h)]
    schur = [[None] * h for _ in range(h)]
    for i in range(h):
        for j in range(i, h):
            schur[i][j] = p[h + i][h + j] - sum(side[k][i] * ts[k][j] for k in range(h))
            schur[j][i] = schur[i][j]
    si = block_inverse(schur)
    tss = [[sum(ts[i][k] * si[k][j] for k in range(h)) for j in range(h)] for i in range(h)]
    out = [[None] * m for _ in range(m)]
    for i in range(h):
        for j in range(h):
            out[i][h + j] = -tss[i][j]
            out[h + j][i] = -tss[i][j]
            out[h + i][h + j] = si[i][j]
            if j >= i:
                out[i][j] = ti[i][j] + sum(tss[i][k] * ts[j][k] for k in range(h))
                out[j][i] = out[i][j]
    return out


def total(values):
    values = list(values)
    while len(values) > 1:
        values = [values[i] + values[i + 1] if i + 1 < len(values) else values[i] for i in range(0, len(values), 2)]
    return values[0]


def sweep_inverse(tiles):
    n = tiles[0].shape[1]
    full = (SUB, n)
    lane = lax.broadcasted_iota(jnp.int32, (1, n), 1)
    sub = lax.broadcasted_iota(jnp.int32, (SUB, 1), 0)
    for t in range(n // SUB):
        k = t * SUB
        inside = (lane >= k) & (lane < k + SUB)
        rows = [tiles[t][u : u + 1, :] for u in range(SUB)]
        cols = [[jnp.broadcast_to(x[:, k + u : k + u + 1], full) for u in range(SUB)] for x in tiles]
        piv = [[cols[t][v][u : u + 1, :] for v in range(SUB)] for u in range(SUB)]
        inv = block_inverse(piv)
        rows = [jnp.where(inside, (lane == k + u).astype(jnp.float32), rows[u]) for u in range(SUB)]
        w = [total(inv[u][v] * rows[v] for v in range(SUB)) for u in range(SUB)]
        new = []
        for i, x in enumerate(tiles):
            if i == t:
                y = jnp.broadcast_to(w[0], full)
                for u in range(1, SUB):
                    y = jnp.where(sub == u, w[u], y)
            else:
                y = jnp.where(inside, 0.0, x) - total(cols[i][u] * w[u] for u in range(SUB))
            new.append(y)
        tiles = new
    return tiles


def split(x):
    high = x.astype(jnp.bfloat16)
    return high, (x - high.astype(jnp.float32)).astype(jnp.bfloat16)


def dot3(a, b, contract=((1,), (0,))):
    a_high, a_low = split(a)
    b_high, b_low = split(b)

    def one(x, y):
        return lax.dot_general(x, y, (contract, ((), ())), preferred_element_type=jnp.float32)

    return one(a_high, b_high) + (one(a_high, b_low) + one(a_low, b_high))


def exact(a, b, contract=((1,), (0,))):
    return lax.dot_general(a, b, (contract, ((), ())), precision=precise, preferred_element_type=jnp.float32)


def whole():
    return pl.BlockSpec(memory_space=pltpu.VMEM)


def scalar():
    return pl.BlockSpec(memory_space=pltpu.SMEM)


def params(mib):
    return pltpu.CompilerParams(vmem_limit_bytes=int(mib * MIB))


def f32(*shape):
    return jax.ShapeDtypeStruct(shape, jnp.float32)


def hot(values, count):
    return (lax.broadcasted_iota(jnp.int32, (count, values.shape[1]), 0) == values).astype(jnp.float32)


def vectors_of(kinds, readout):
    extra = SUB - readout.shape[0]
    table = jnp.concatenate([readout, jnp.zeros((extra, readout.shape[1]), jnp.float32)], axis=0)
    return exact(hot(kinds, SUB), table, ((0,), (0,)))


def layer(atoms, weights, bias, vectors):
    hidden = jnp.tanh(dot3(atoms, weights) + bias)
    return hidden * vectors, (1.0 - hidden * hidden) * vectors


def first_kernel(atoms_ref, kinds_ref, member_ref, weights_ref, bias_ref, readout_ref, out_ref, turned, masked):
    atoms = atoms_ref[...]
    vectors = vectors_of(kinds_ref[0:1, :], readout_ref[...])
    energy, slope = layer(atoms, weights_ref[...], bias_ref[...], vectors)
    group_hot = hot(member_ref[0:1, :], GROUP_LOCAL)
    turned[...] = atoms.T
    for i in range(FEATURES):
        masked[SUB * i : SUB * i + SUB, :] = turned[i : i + 1, :] * group_hot
    grads = dot3(masked[...], slope)
    energies = jnp.sum(dot3(group_hot, energy), axis=1, keepdims=True)
    energies = jnp.broadcast_to(energies, (GROUP_LOCAL, FEATURES))
    blocks, _, wide = out_ref.shape
    per = FEATURES // blocks
    for j in range(blocks):
        for f in range(per):
            i = j * per + f
            out_ref[j, :, f * FEATURES : (f + 1) * FEATURES] = grads[SUB * i : SUB * i + SUB]
        out_ref[j, :, wide - FEATURES :] = energies


def first_terms(atoms, kinds, member, weights, bias, readout, cols, width):
    local = atoms.shape[1]
    return pl.pallas_call(
        first_kernel,
        grid=(1,),
        out_shape=f32(cols, GROUP_LOCAL, width + FEATURES),
        in_specs=[pl.BlockSpec((None, local, FEATURES), lambda n: (0, 0, 0))] + [whole()] * 5,
        out_specs=whole(),
        scratch_shapes=[pltpu.VMEM((FEATURES, local), jnp.float32), pltpu.VMEM((SUB * FEATURES, local), jnp.float32)],
        compiler_params=params(63.9),
        name="first_terms",
    )(atoms, kinds, member, weights, bias, readout)


def prepare_kernel(col_ref, gathered_ref, readout_ref, vectors_ref, masked_ref, turned):
    local = vectors_ref.shape[0]
    lines = local // FEATURES
    count = (masked_ref.shape[0] - GROUP_LOCAL) // GROUP_LOCAL

    def row(start):
        parts = [gathered_ref[start + u : start + u + 1, :] for u in range(lines)]
        return jnp.concatenate(parts, axis=1).astype(jnp.int32)

    vectors_ref[...] = vectors_of(row(local), readout_ref[...])
    group_hot = hot(row(local + lines), GROUP_LOCAL)
    turned[...] = gathered_ref[:local, :].T
    part = turned[pl.ds(pl.multiple_of(col_ref[0] * count, SUB), count), :]
    for f in range(count):
        masked_ref[SUB * f : SUB * f + SUB, :] = part[f : f + 1, :] * group_hot
    masked_ref[SUB * count :, :] = group_hot


def prepare(gathered, readout, col_index, local, count):
    cols, tall, _ = gathered.shape
    lines = GROUP_LOCAL * (count + 1)
    return pl.pallas_call(
        prepare_kernel,
        grid=(cols,),
        out_shape=(f32(cols * local, FEATURES), f32(lines, cols * local)),
        in_specs=[scalar(), pl.BlockSpec((None, tall, FEATURES), lambda n: (n, 0, 0)), whole()],
        out_specs=(pl.BlockSpec((local, FEATURES), lambda n: (n, 0)), pl.BlockSpec((lines, local), lambda n: (0, n))),
        scratch_shapes=[pltpu.VMEM((FEATURES, local), jnp.float32)],
        compiler_params=params(63),
        name="prepare_terms",
    )(col_index, gathered, readout)


def later_kernel(gathered_ref, vectors_ref, masked_ref, weights_ref, change_ref, bias_ref, out_ref, acc):
    step = pl.program_id(0)
    blocks = gathered_ref.shape[0]
    local = vectors_ref.shape[0] // blocks
    atoms = gathered_ref[:, :local, :].reshape(blocks * local, FEATURES)
    weights = weights_ref[...] + change_ref[...].reshape(FEATURES, FEATURES)
    energy, slope = layer(atoms, weights, bias_ref[...], vectors_ref[...])
    split_row = acc.shape[0] - GROUP_LOCAL
    grads = dot3(masked_ref[:split_row, :], slope)
    energies = dot3(masked_ref[split_row:, :], energy)

    @pl.when(step == 0)
    def _():
        acc[:split_row, :] = grads
        acc[split_row:, :] = energies

    @pl.when(step > 0)
    def _():
        acc[:split_row, :] += grads
        acc[split_row:, :] += energies

    @pl.when(step == pl.num_programs(0) - 1)
    def _():
        total_energy = jnp.sum(acc[split_row:, :], axis=1, keepdims=True)
        total_energy = jnp.broadcast_to(total_energy, (GROUP_LOCAL, FEATURES))
        for copy in range(out_ref.shape[0]):
            for f in range(split_row // SUB):
                out_ref[copy, :, f * FEATURES : (f + 1) * FEATURES] = acc[SUB * f : SUB * f + SUB, :]
            out_ref[copy, :, split_row // SUB * FEATURES :] = total_energy


def later_terms(gathered, vectors, masked, weights, change, bias, copies):
    cols, tall, _ = gathered.shape
    parts = 4
    local = vectors.shape[0] // cols
    lines = masked.shape[0]
    width = (lines // GROUP_LOCAL - 1) * FEATURES
    each = cols // parts
    return pl.pallas_call(
        later_kernel,
        grid=(parts,),
        out_shape=f32(copies, GROUP_LOCAL, width + FEATURES),
        in_specs=[
            pl.BlockSpec((each, tall, FEATURES), lambda n: (n, 0, 0)),
            pl.BlockSpec((each * local, FEATURES), lambda n: (n, 0)),
            pl.BlockSpec((lines, each * local), lambda n: (0, n)),
            whole(),
            whole(),
            whole(),
        ],
        out_specs=whole(),
        scratch_shapes=[pltpu.VMEM((lines, FEATURES), jnp.float32)],
        compiler_params=params(63),
        name="later_terms",
    )(gathered, vectors, masked, weights, change, bias)


def sum_kernel(x_ref, out_ref):
    out = total(x_ref[i] for i in range(x_ref.shape[0]))
    for copy in range(out_ref.shape[0]):
        out_ref[copy] = out


def sum_copies(x, copies):
    return pl.pallas_call(
        sum_kernel,
        out_shape=f32(copies, *x.shape[1:]),
        in_specs=[whole()],
        out_specs=whole(),
        compiler_params=params(8),
        name="sum_of_chunks",
    )(x)


def terms_kernel(old, side_ref, jac_ref, cov_ref, *rest):
    width = cov_ref.shape[1]
    if old:
        scaled_ref, gains_ref = rest[:2]
        out_ref, moved = rest[-2:]
    else:
        out_ref = rest[-1]
    jac = jac_ref[:, :, :width].reshape(-1, width)
    terms = dot3(jac, cov_ref[...], ((1,), (1,)))
    if old:

        @pl.when(pl.program_id(0) == 0)
        def _():
            moved[...] = exact(jac, scaled_ref[...], ((1,), (1,)))

        terms = (terms - exact(moved[...], gains_ref[...])) * (1.0 / forget_rate)
    out_ref[...] = terms.reshape(out_ref.shape)


def gain_terms(side, jac, cov, old, into):
    blocks, sub, wide = jac.shape
    rows, width = cov.shape
    part = 256
    ins = [
        pl.BlockSpec((blocks, sub, wide), lambda n, s: (0, 0, 0)),
        pl.BlockSpec((part, width), lambda n, s: (n, 0)),
    ]
    args = [jac, cov]
    scratch = []
    if old:
        scaled, gains = old
        ins += [
            pl.BlockSpec(scaled.shape, lambda n, s: (0, 0)),
            pl.BlockSpec((gains.shape[0], part), lambda n, s: (0, n)),
        ]
        args += [scaled, gains]
        scratch = [pltpu.VMEM((blocks * sub, scaled.shape[0]), jnp.float32)]
    alias = {}
    if into is not None:
        ins.append(pl.BlockSpec(memory_space=pl.ANY))
        args.append(into)
        alias = {len(args): 0}
    return pl.pallas_call(
        functools.partial(terms_kernel, bool(old)),
        grid_spec=pltpu.PrefetchScalarGridSpec(
            num_scalar_prefetch=1,
            grid=(rows // part,),
            in_specs=ins,
            out_specs=pl.BlockSpec((blocks, sub, part), lambda n, s: (s[0], 0, n)),
            scratch_shapes=scratch,
        ),
        out_shape=f32(2 * blocks, sub, rows),
        input_output_aliases=alias,
        compiler_params=params(60.1),
        name="gain_terms",
    )(side, *args)


def part_kernel(side_ref, own_ref, other_ref, gains_ref, out_ref, jac):
    half = own_ref.shape[0]
    width = gains_ref.shape[1]
    side = side_ref[0]
    jac[pl.ds(side * half, half)] = own_ref[:, :, :width]
    jac[pl.ds((1 - side) * half, half)] = other_ref[:, :, :width]
    part = exact(gains_ref[...], jac[...].reshape(-1, width), ((1,), (1,)))
    for copy in range(out_ref.shape[0]):
        out_ref[copy] = part


def innovation_part(side, own, other, gains, copies):
    half, sub, _ = own.shape
    width = gains.shape[1]
    return pl.pallas_call(
        part_kernel,
        out_shape=f32(copies, sub, 2 * half * sub),
        in_specs=[scalar(), whole(), whole(), whole()],
        out_specs=whole(),
        scratch_shapes=[pltpu.VMEM((2 * half, sub, width), jnp.float32)],
        compiler_params=params(8),
        name="innovation_part",
    )(side, own, other, gains)


def pack_kernel(parts_ref, gains_ref, out_ref):
    width = gains_ref.shape[1]
    part = total(parts_ref[i] for i in range(parts_ref.shape[0]))
    for copy in range(out_ref.shape[0]):
        out_ref[copy, :, :width] = gains_ref[...]
        out_ref[copy, :, width:] = part


def pack(parts, gains, copies):
    sub, width = gains.shape
    return pl.pallas_call(
        pack_kernel,
        out_shape=f32(copies, sub, width + parts.shape[2]),
        in_specs=[whole(), whole()],
        out_specs=whole(),
        compiler_params=params(8),
        name="pack_gains",
    )(parts, gains)


def update_kernel(
    order, side_ref, own_ref, other_ref, e_own_ref, e_other_ref, targets_ref, inverse_ref, gains_ref, change_ref, both, energy
):
    n = targets_ref.shape[0]
    width = own_ref.shape[2] - n
    half = own_ref.shape[0]
    side = side_ref[0]
    mine, theirs = pl.ds(side * half, half), pl.ds((1 - side) * half, half)
    both[mine] = own_ref[...]
    both[theirs] = other_ref[...]
    energy[mine] = e_own_ref[...]
    energy[theirs] = e_other_ref[...]
    places = [order.index(t) for t in range(n // SUB)]
    curvature = jnp.concatenate([both[p, :, width:] for p in places], axis=0)
    row = lax.broadcasted_iota(jnp.int32, (n, n), 0)
    col = lax.broadcasted_iota(jnp.int32, (n, n), 1)
    innovation = 0.5 * (curvature + curvature.T) + jnp.where(row == col, forget_rate, 0.0)
    tiles = sweep_inverse([innovation[SUB * i : SUB * i + SUB] for i in range(n // SUB)])
    weighted = []
    for i, x in enumerate(tiles):
        inverse_ref[SUB * i : SUB * i + SUB, :] = x
        weighted.append(x * (targets_ref[SUB * i : SUB * i + SUB, :] - energy[i]))
    coefficient = jnp.broadcast_to(jnp.sum(total(weighted), axis=0, keepdims=True), (SUB, n))
    gains = jnp.concatenate([both[p, :, :width] for p in places], axis=0)
    gains_ref[...] = gains
    moved = exact(coefficient, gains)
    sub = lax.broadcasted_iota(jnp.int32, (SUB, FEATURES), 0)
    change = moved[:, :FEATURES]
    for r in range(1, width // FEATURES):
        change = jnp.where(sub == r, moved[:, r * FEATURES : (r + 1) * FEATURES], change)
    for j in range(change_ref.shape[0]):
        change_ref[j] = change


def solve_update(side, own, other, jac_own, jac_other, targets, copies, order):
    n = targets.shape[0]
    half, sub, wide = own.shape
    last = jac_own.shape[2] // FEATURES - 1
    energies = pl.BlockSpec((half, sub, FEATURES), lambda i: (0, 0, last))
    return pl.pallas_call(
        functools.partial(update_kernel, order),
        grid=(1,),
        out_shape=(f32(n, n), f32(n, wide - n), f32(copies, SUB, FEATURES)),
        in_specs=[scalar(), whole(), whole(), energies, energies, whole()],
        out_specs=(whole(), whole(), whole()),
        scratch_shapes=[pltpu.VMEM((2 * half, sub, wide), jnp.float32), pltpu.VMEM((2 * half, sub, FEATURES), jnp.float32)],
        compiler_params=params(8),
        name="inverse_and_change",
    )(side, own, other, jac_own, jac_other, targets)


def exchange(chunks, axis):
    return lax.all_to_all(chunks, axis, 0, 0, tiled=True)


def gather_pair(copies):
    count = copies.shape[0]
    lanes = [[core + 2 * z for z in range(count)] for core in range(2)]
    own = lax.all_to_all(copies, "grp", 0, 0, tiled=True, axis_index_groups=lanes)
    other = lax.ppermute(own, "grp", [(i, i ^ 1) for i in range(2 * count)])
    return own, other


def far_row(j, side):
    return (j // side + side // 2) % side * side + (j % side + side // 2) % side


def swap(x, chunk_of_row):
    size = len(chunk_of_row)
    pairs = [(i * size + chunk_of_row[a], a * size + i) for i in range(size) for a in range(size)]
    return lax.ppermute(x, ("grp", "atm"), pairs)


def gather_rows(own):
    twice = jnp.concatenate([own, own], axis=0)
    got = lax.all_gather(twice, "atm", axis=0, tiled=False)
    return got[:, : own.shape[0]].reshape(-1, own.shape[1])


def gather_kernel(atoms_ref, kinds_ref, member_ref, out_ref):
    local = atoms_ref.shape[0]
    lines = local // FEATURES
    out_ref[:local, :] = atoms_ref[...]
    out_ref[local:, :] = jnp.zeros((out_ref.shape[0] - local, FEATURES), jnp.float32)
    for which, ref in enumerate((kinds_ref, member_ref)):
        for u in range(lines):
            values = ref[1:2, u * FEATURES : (u + 1) * FEATURES].astype(jnp.float32)
            place = local + which * lines + u
            out_ref[place : place + 1, :] = values


def gather_atoms(atoms, kinds, member):
    local = atoms.shape[1]
    packed = pl.pallas_call(
        gather_kernel,
        grid=(1,),
        out_shape=f32(local + SUB, FEATURES),
        in_specs=[pl.BlockSpec((None, local, FEATURES), lambda n: (1, 0, 0)), whole(), whole()],
        out_specs=whole(),
        compiler_params=params(63.9),
        name="atoms_with_types",
    )(atoms, kinds, member)
    return lax.all_gather(packed, "atm", axis=0, tiled=False)


def together(*values):
    return lax.optimization_barrier(values)


def body(atoms, kinds, member, targets, weights, bias, readout, covariance):
    rows, cols = lax.axis_size("grp"), lax.axis_size("atm")
    chips = rows // 2
    col_index = lax.axis_index("atm").reshape(1)
    side = (lax.axis_index("grp") % 2).reshape(1)
    away = 1 - side
    local = atoms.shape[1]
    groups = GROUP_LOCAL * rows
    width = covariance.shape[1]
    bias = bias.reshape(1, FEATURES)
    ordered = targets.reshape(STEPS, chips, 2, GROUP_LOCAL).transpose(0, 2, 1, 3).reshape(STEPS, groups, 1)
    ordered = jnp.broadcast_to(ordered, (STEPS, groups, FEATURES))
    chunk_of_row = [far_row(a, math.isqrt(rows)) for a in range(rows)]
    order = [chunk_of_row[2 * z + core] for core in range(2) for z in range(chips)]
    current = weights
    row_gains, scaled = [], []
    for step in range(STEPS):
        if step == 0:
            chunks = first_terms(atoms, kinds, member, current, bias, readout, cols, width)
            chunks, later = together(chunks, atoms)
            gathered = gather_atoms(later, kinds, member)
            copies = sum_copies(exchange(chunks, "atm"), chips)
        else:
            copies = later_terms(gathered, vectors, masked, weights, change, bias, chips)
        jac_own, jac_other = gather_pair(copies)
        old = (scaled[0], row_gains[0]) if step else None
        terms = gain_terms(side, jac_own, covariance, old, None)
        terms = gain_terms(away, jac_other, covariance, old, terms)
        own = exchange(terms, "atm").sum(axis=0)
        if step == 0:
            own, gathered, ordered = together(own, gathered, ordered)
        row_gains.append(gather_rows(own))
        other = swap(own, chunk_of_row)
        if step == 0:
            vectors, masked = prepare(gathered, readout, col_index, local, width // FEATURES)
            other, vectors, masked = together(other, vectors, masked)
        part = exchange(innovation_part(side, jac_own, jac_other, other, cols), "atm")
        got_own, got_other = gather_pair(pack(part, other, chips))
        inverse, col_gains, change = solve_update(
            side, got_own, got_other, jac_own, jac_other, ordered[step], cols, order
        )
        if step == STEPS - 1:
            change, *row_gains = together(change, *row_gains)
        change = exchange(change, "atm")
        current = current + change.reshape(FEATURES, FEATURES)
        scaled.append(dot(inverse, col_gains, ((1,), (0,)), precise))
    left = jnp.concatenate(row_gains, axis=0)
    right = jnp.concatenate([x / forget_rate ** (STEPS - i) for i, x in enumerate(scaled)], axis=0)
    covar = covariance / forget_rate**STEPS - dot(left, right, ((0,), (0,)), three)
    return (covar, current)


def solution(mesh):
    return jax.shard_map(
        body,
        mesh=mesh,
        in_specs=(
            P(None, ("grp", "atm"), None),
            P(None, ("grp", "atm")),
            P(None, ("grp", "atm")),
            P(),
            P(),
            P(),
            P(),
            P("grp", "atm"),
        ),
        out_specs=(P("grp", "atm"), P()),
        check_vma=False,
    )
```

```python
import functools
import math

import jax
import jax.numpy as jnp
from jax import lax
from jax.experimental import pallas as pl
from jax.experimental.pallas import tpu as pltpu
from jax.sharding import PartitionSpec as P

FEATURES = 128
GROUP_LOCAL = 8
STEPS = 2
SUB = 8

forget_rate = 0.98
precise = lax.Precision.HIGHEST
three = lax.Precision.HIGH
MIB = 1024 * 1024


def dot(a, b, contract, precision):
    return lax.dot_general(
        a, b, ((contract[0], contract[1]), ((), ())), precision=precision, preferred_element_type=jnp.float32
    )


def block_inverse(p):
    m = len(p)
    if m == 1:
        return [[1.0 / p[0][0]]]
    if m == 2:
        a, b, d = p[0][0], p[0][1], p[1][1]
        r = 1.0 / (a * d - b * b)
        return [[d * r, -b * r], [-b * r, a * r]]
    h = m // 2
    top = [[p[i][j] for j in range(h)] for i in range(h)]
    side = [[p[i][h + j] for j in range(h)] for i in range(h)]
    ti = block_inverse(top)
    ts = [[sum(ti[i][k] * side[k][j] for k in range(h)) for j in range(h)] for i in range(h)]
    schur = [[None] * h for _ in range(h)]
    for i in range(h):
        for j in range(i, h):
            schur[i][j] = p[h + i][h + j] - sum(side[k][i] * ts[k][j] for k in range(h))
            schur[j][i] = schur[i][j]
    si = block_inverse(schur)
    tss = [[sum(ts[i][k] * si[k][j] for k in range(h)) for j in range(h)] for i in range(h)]
    out = [[None] * m for _ in range(m)]
    for i in range(h):
        for j in range(h):
            out[i][h + j] = -tss[i][j]
            out[h + j][i] = -tss[i][j]
            out[h + i][h + j] = si[i][j]
            if j >= i:
                out[i][j] = ti[i][j] + sum(tss[i][k] * ts[j][k] for k in range(h))
                out[j][i] = out[i][j]
    return out


def total(values):
    values = list(values)
    while len(values) > 1:
        values = [values[i] + values[i + 1] if i + 1 < len(values) else values[i] for i in range(0, len(values), 2)]
    return values[0]


def sweep_inverse(tiles):
    n = tiles[0].shape[1]
    full = (SUB, n)
    lane = lax.broadcasted_iota(jnp.int32, (1, n), 1)
    sub = lax.broadcasted_iota(jnp.int32, (SUB, 1), 0)
    for t in range(n // SUB):
        k = t * SUB
        inside = (lane >= k) & (lane < k + SUB)
        rows = [tiles[t][u : u + 1, :] for u in range(SUB)]
        cols = [[jnp.broadcast_to(x[:, k + u : k + u + 1], full) for u in range(SUB)] for x in tiles]
        piv = [[cols[t][v][u : u + 1, :] for v in range(SUB)] for u in range(SUB)]
        inv = block_inverse(piv)
        rows = [jnp.where(inside, (lane == k + u).astype(jnp.float32), rows[u]) for u in range(SUB)]
        w = [total(inv[u][v] * rows[v] for v in range(SUB)) for u in range(SUB)]
        new = []
        for i, x in enumerate(tiles):
            if i == t:
                y = jnp.broadcast_to(w[0], full)
                for u in range(1, SUB):
                    y = jnp.where(sub == u, w[u], y)
            else:
                y = jnp.where(inside, 0.0, x) - total(cols[i][u] * w[u] for u in range(SUB))
            new.append(y)
        tiles = new
    return tiles


def split(x):
    high = x.astype(jnp.bfloat16)
    return high, (x - high.astype(jnp.float32)).astype(jnp.bfloat16)


def dot3(a, b, contract=((1,), (0,))):
    a_high, a_low = split(a)
    b_high, b_low = split(b)

    def one(x, y):
        return lax.dot_general(x, y, (contract, ((), ())), preferred_element_type=jnp.float32)

    return one(a_high, b_high) + (one(a_high, b_low) + one(a_low, b_high))


def exact(a, b, contract=((1,), (0,))):
    return lax.dot_general(a, b, (contract, ((), ())), precision=precise, preferred_element_type=jnp.float32)


def whole():
    return pl.BlockSpec(memory_space=pltpu.VMEM)


def scalar():
    return pl.BlockSpec(memory_space=pltpu.SMEM)


def params(mib):
    return pltpu.CompilerParams(vmem_limit_bytes=int(mib * MIB))


def f32(*shape):
    return jax.ShapeDtypeStruct(shape, jnp.float32)


def hot(values, count):
    return (lax.broadcasted_iota(jnp.int32, (count, values.shape[1]), 0) == values).astype(jnp.float32)


def vectors_of(kinds, readout):
    extra = 2 * SUB - readout.shape[0]
    table = jnp.concatenate([readout, jnp.zeros((extra, readout.shape[1]), jnp.float32)], axis=0)
    which = hot(kinds, 2 * SUB).astype(jnp.bfloat16)
    out = 0.0
    for _ in range(3):
        part = table.astype(jnp.bfloat16)
        table = table - part.astype(jnp.float32)
        out = out + lax.dot_general(which, part, (((0,), (0,)), ((), ())), preferred_element_type=jnp.float32)
    return out


def layer(atoms, weights, bias, vectors):
    hidden = jnp.tanh(dot3(atoms, weights) + bias)
    return hidden * vectors, (1.0 - hidden * hidden) * vectors


def first_kernel(atoms_ref, kinds_ref, member_ref, weights_ref, bias_ref, readout_ref, out_ref, turned, masked):
    atoms = atoms_ref[...]
    vectors = vectors_of(kinds_ref[0:1, :], readout_ref[...])
    energy, slope = layer(atoms, weights_ref[...], bias_ref[...], vectors)
    group_hot = hot(member_ref[0:1, :], GROUP_LOCAL)
    turned[...] = atoms.T
    for i in range(FEATURES):
        masked[SUB * i : SUB * i + SUB, :] = turned[i : i + 1, :] * group_hot
    grads = dot3(masked[...], slope)
    energies = jnp.sum(dot3(group_hot, energy), axis=1, keepdims=True)
    energies = jnp.broadcast_to(energies, (GROUP_LOCAL, FEATURES))
    blocks, _, wide = out_ref.shape
    per = FEATURES // blocks
    for j in range(blocks):
        for f in range(per):
            i = j * per + f
            out_ref[j, :, f * FEATURES : (f + 1) * FEATURES] = grads[SUB * i : SUB * i + SUB]
        out_ref[j, :, wide - FEATURES :] = energies


def first_terms(atoms, kinds, member, weights, bias, readout, cols, width):
    local = atoms.shape[1]
    return pl.pallas_call(
        first_kernel,
        grid=(1,),
        out_shape=f32(cols, GROUP_LOCAL, width + FEATURES),
        in_specs=[pl.BlockSpec((None, local, FEATURES), lambda n: (0, 0, 0))] + [whole()] * 5,
        out_specs=whole(),
        scratch_shapes=[pltpu.VMEM((FEATURES, local), jnp.float32), pltpu.VMEM((SUB * FEATURES, local), jnp.float32)],
        compiler_params=params(63.9),
        name="first_terms",
    )(atoms, kinds, member, weights, bias, readout)


def prepare_kernel(col_ref, gathered_ref, readout_ref, vectors_ref, masked_ref, turned):
    blocks = gathered_ref.shape[0]
    local = vectors_ref.shape[0] // blocks
    lines = local // FEATURES
    count = (masked_ref.shape[0] - GROUP_LOCAL) // GROUP_LOCAL
    first = pl.multiple_of(col_ref[0] * count, SUB)
    for block in range(blocks):

        def row(start):
            parts = [gathered_ref[block, start + u : start + u + 1, :] for u in range(lines)]
            return jnp.concatenate(parts, axis=1).astype(jnp.int32)

        here = slice(block * local, (block + 1) * local)
        vectors_ref[here, :] = vectors_of(row(local), readout_ref[...])
        group_hot = hot(row(local + lines), GROUP_LOCAL)
        turned[block] = gathered_ref[block, :local, :].T
        part = turned[block, pl.ds(first, count), :]
        for f in range(count):
            masked_ref[SUB * f : SUB * f + SUB, here] = part[f : f + 1, :] * group_hot
        masked_ref[SUB * count :, here] = group_hot


def prepare(gathered, readout, col_index, local, count):
    cols, tall, _ = gathered.shape
    lines = GROUP_LOCAL * (count + 1)
    parts = 4
    each = cols // parts
    return pl.pallas_call(
        prepare_kernel,
        grid=(parts,),
        out_shape=(f32(cols * local, FEATURES), f32(lines, cols * local)),
        in_specs=[scalar(), pl.BlockSpec((each, tall, FEATURES), lambda n: (n, 0, 0)), whole()],
        out_specs=(
            pl.BlockSpec((each * local, FEATURES), lambda n: (n, 0)),
            pl.BlockSpec((lines, each * local), lambda n: (0, n)),
        ),
        scratch_shapes=[pltpu.VMEM((each, FEATURES, local), jnp.float32)],
        compiler_params=params(63),
        name="prepare_terms",
    )(col_index, gathered, readout)


def later_kernel(gathered_ref, vectors_ref, masked_ref, weights_ref, change_ref, bias_ref, out_ref, acc):
    step = pl.program_id(0)
    blocks = gathered_ref.shape[0]
    local = vectors_ref.shape[0] // blocks
    atoms = gathered_ref[:, :local, :].reshape(blocks * local, FEATURES)
    weights = weights_ref[...] + change_ref[...].reshape(FEATURES, FEATURES)
    energy, slope = layer(atoms, weights, bias_ref[...], vectors_ref[...])
    split_row = acc.shape[0] - GROUP_LOCAL
    grads = dot3(masked_ref[:split_row, :], slope)
    energies = dot3(masked_ref[split_row:, :], energy)

    @pl.when(step == 0)
    def _():
        acc[:split_row, :] = grads
        acc[split_row:, :] = energies

    @pl.when(step > 0)
    def _():
        acc[:split_row, :] += grads
        acc[split_row:, :] += energies

    @pl.when(step == pl.num_programs(0) - 1)
    def _():
        total_energy = jnp.sum(acc[split_row:, :], axis=1, keepdims=True)
        total_energy = jnp.broadcast_to(total_energy, (GROUP_LOCAL, FEATURES))
        for copy in range(out_ref.shape[0]):
            for f in range(split_row // SUB):
                out_ref[copy, :, f * FEATURES : (f + 1) * FEATURES] = acc[SUB * f : SUB * f + SUB, :]
            out_ref[copy, :, split_row // SUB * FEATURES :] = total_energy


def later_terms(gathered, vectors, masked, weights, change, bias, copies):
    cols, tall, _ = gathered.shape
    parts = 4
    local = vectors.shape[0] // cols
    lines = masked.shape[0]
    width = (lines // GROUP_LOCAL - 1) * FEATURES
    each = cols // parts
    return pl.pallas_call(
        later_kernel,
        grid=(parts,),
        out_shape=f32(copies, GROUP_LOCAL, width + FEATURES),
        in_specs=[
            pl.BlockSpec((each, tall, FEATURES), lambda n: (n, 0, 0)),
            pl.BlockSpec((each * local, FEATURES), lambda n: (n, 0)),
            pl.BlockSpec((lines, each * local), lambda n: (0, n)),
            whole(),
            whole(),
            whole(),
        ],
        out_specs=whole(),
        scratch_shapes=[pltpu.VMEM((lines, FEATURES), jnp.float32)],
        compiler_params=params(63),
        name="later_terms",
    )(gathered, vectors, masked, weights, change, bias)


def pack_kernel(parts_ref, gains_ref, out_ref):
    width = gains_ref.shape[1]
    part = total(parts_ref[i] for i in range(parts_ref.shape[0]))
    for copy in range(out_ref.shape[0]):
        out_ref[copy, :, :width] = gains_ref[...]
        out_ref[copy, :, width:] = part


def pack(parts, gains, copies):
    sub, width = gains.shape
    return pl.pallas_call(
        pack_kernel,
        out_shape=f32(copies, sub, width + parts.shape[2]),
        in_specs=[whole(), whole()],
        out_specs=whole(),
        compiler_params=params(8),
        name="pack_gains",
    )(parts, gains)


def update_kernel(order, side_ref, own_ref, other_ref, energy_ref, targets_ref, inverse_ref, gains_ref, change_ref, both):
    n = targets_ref.shape[0]
    width = own_ref.shape[2] - n
    half = own_ref.shape[0]
    side = side_ref[0]
    both[pl.ds(side * half, half)] = own_ref[...]
    both[pl.ds((1 - side) * half, half)] = other_ref[...]
    places = [order.index(t) for t in range(n // SUB)]
    curvature = jnp.concatenate([both[p, :, width:] for p in places], axis=0)
    row = lax.broadcasted_iota(jnp.int32, (n, n), 0)
    col = lax.broadcasted_iota(jnp.int32, (n, n), 1)
    innovation = 0.5 * (curvature + curvature.T) + jnp.where(row == col, forget_rate, 0.0)
    tiles = sweep_inverse([innovation[SUB * i : SUB * i + SUB] for i in range(n // SUB)])
    weighted = []
    for i, x in enumerate(tiles):
        here = slice(SUB * i, SUB * i + SUB)
        inverse_ref[here, :] = x
        weighted.append(x * (targets_ref[here, :] - energy_ref[here, :]))
    coefficient = jnp.broadcast_to(jnp.sum(total(weighted), axis=0, keepdims=True), (SUB, n))
    gains = jnp.concatenate([both[p, :, :width] for p in places], axis=0)
    gains_ref[...] = gains
    moved = exact(coefficient, gains)
    sub = lax.broadcasted_iota(jnp.int32, (SUB, FEATURES), 0)
    change = moved[:, :FEATURES]
    for r in range(1, width // FEATURES):
        change = jnp.where(sub == r, moved[:, r * FEATURES : (r + 1) * FEATURES], change)
    for j in range(change_ref.shape[0]):
        change_ref[j] = change


def solve_update(side, own, other, stacked, targets, copies, order):
    n = targets.shape[0]
    half, sub, wide = own.shape
    last = stacked.shape[1] // FEATURES - 1
    return pl.pallas_call(
        functools.partial(update_kernel, order),
        grid=(1,),
        out_shape=(f32(n, n), f32(n, wide - n), f32(copies, SUB, FEATURES)),
        in_specs=[scalar(), whole(), whole(), pl.BlockSpec((n, FEATURES), lambda i: (0, last)), whole()],
        out_specs=(whole(), whole(), whole()),
        scratch_shapes=[pltpu.VMEM((2 * half, sub, wide), jnp.float32)],
        compiler_params=params(8),
        name="inverse_and_change",
    )(side, own, other, stacked, targets)


def exchange(chunks, axis):
    return lax.all_to_all(chunks, axis, 0, 0, tiled=True)


def spread(x, axis):
    return exchange(jnp.broadcast_to(x[None], (lax.axis_size(axis),) + x.shape), axis)


def gather_pair(copies):
    count = copies.shape[0]
    lanes = [[core + 2 * z for z in range(count)] for core in range(2)]
    own = lax.all_to_all(copies, "grp", 0, 0, tiled=True, axis_index_groups=lanes)
    other = lax.ppermute(own, "grp", [(i, i ^ 1) for i in range(2 * count)])
    return own, other


def far_row(j, side):
    return (j // side + side // 2) % side * side + (j % side + side // 2) % side


def swap(x, chunk_of_row):
    size = len(chunk_of_row)
    pairs = [(i * size + chunk_of_row[a], a * size + i) for i in range(size) for a in range(size)]
    return lax.ppermute(x, ("grp", "atm"), pairs)


def gather_rows(own):
    twice = jnp.concatenate([own, own], axis=0)
    got = lax.all_gather(twice, "atm", axis=0, tiled=False)
    return got[:, : own.shape[0]].reshape(-1, own.shape[1])


def gather_kernel(atoms_ref, kinds_ref, member_ref, out_ref):
    local = atoms_ref.shape[0]
    lines = local // FEATURES
    out_ref[:local, :] = atoms_ref[...]
    out_ref[local:, :] = jnp.zeros((out_ref.shape[0] - local, FEATURES), jnp.float32)
    for which, ref in enumerate((kinds_ref, member_ref)):
        for u in range(lines):
            values = ref[1:2, u * FEATURES : (u + 1) * FEATURES].astype(jnp.float32)
            place = local + which * lines + u
            out_ref[place : place + 1, :] = values


def gather_atoms(atoms, kinds, member):
    local = atoms.shape[1]
    packed = pl.pallas_call(
        gather_kernel,
        grid=(1,),
        out_shape=f32(local + SUB, FEATURES),
        in_specs=[pl.BlockSpec((None, local, FEATURES), lambda n: (1, 0, 0)), whole(), whole()],
        out_specs=whole(),
        compiler_params=params(63.9),
        name="atoms_with_types",
    )(atoms, kinds, member)
    return lax.all_gather(packed, "atm", axis=0, tiled=False)


def together(*values):
    return lax.optimization_barrier(values)


def body(atoms, kinds, member, targets, weights, bias, readout, covariance):
    rows, cols = lax.axis_size("grp"), lax.axis_size("atm")
    chips = rows // 2
    col_index = lax.axis_index("atm").reshape(1)
    side = (lax.axis_index("grp") % 2).reshape(1)
    local = atoms.shape[1]
    groups = GROUP_LOCAL * rows
    width = covariance.shape[1]
    bias = bias.reshape(1, FEATURES)
    ordered = jnp.broadcast_to(targets[:, :, None], (STEPS, groups, FEATURES))
    chunk_of_row = [far_row(a, math.isqrt(rows)) for a in range(rows)]
    order = [chunk_of_row[2 * z + core] for core in range(2) for z in range(chips)]
    current = weights
    row_gains, scaled = [], []
    for step in range(STEPS):
        if step == 0:
            chunks = first_terms(atoms, kinds, member, current, bias, readout, cols, width)
            chunks, later = together(chunks, atoms)
            gathered = gather_atoms(later, kinds, member)
            chunk = exchange(chunks, "atm").sum(axis=0)
        else:
            chunk = later_terms(gathered, vectors, masked, weights, change, bias, 1)[0]
        stacked = lax.all_gather(chunk, "grp", axis=0, tiled=True)
        jac = stacked[:, :width]
        terms = dot(jac, covariance, ((1,), (1,)), three)
        for gains, part in zip(row_gains, scaled):
            terms = (terms - dot(dot(jac, part, ((1,), (1,)), precise), gains, ((1,), (0,)), precise)) / forget_rate
        own = exchange(terms.reshape(cols, groups // cols, width), "atm").sum(axis=0)
        if step == 0:
            own, gathered, ordered = together(own, gathered, ordered)
        row_gains.append(gather_rows(own))
        other = swap(own, chunk_of_row)
        if step == 0:
            vectors, masked = prepare(gathered, readout, col_index, local, width // FEATURES)
            other, vectors, masked = together(other, vectors, masked)
        part = spread(dot(other, jac, ((1,), (1,)), precise), "atm")
        got_own, got_other = gather_pair(pack(part, other, chips))
        inverse, col_gains, change = solve_update(
            side, got_own, got_other, stacked, ordered[step], cols, order
        )
        if step == STEPS - 1:
            change, *row_gains = together(change, *row_gains)
        change = exchange(change, "atm")
        current = current + change.reshape(FEATURES, FEATURES)
        scaled.append(dot(inverse, col_gains, ((1,), (0,)), precise))
    left = jnp.concatenate(row_gains, axis=0)
    right = jnp.concatenate([x / forget_rate ** (STEPS - i) for i, x in enumerate(scaled)], axis=0)
    covar = covariance / forget_rate**STEPS - dot(left, right, ((0,), (0,)), three)
    return (covar, current)


def solution(mesh):
    return jax.shard_map(
        body,
        mesh=mesh,
        in_specs=(
            P(None, ("grp", "atm"), None),
            P(None, ("grp", "atm")),
            P(None, ("grp", "atm")),
            P(),
            P(),
            P(),
            P(),
            P("grp", "atm"),
        ),
        out_specs=(P("grp", "atm"), P()),
        check_vma=False,
    )
```

```python
import functools
import math

import jax
import jax.numpy as jnp
from jax import lax
from jax.experimental import pallas as pl
from jax.experimental.pallas import tpu as pltpu
from jax.sharding import PartitionSpec as P

FEATURES = 128
GROUP_LOCAL = 8
STEPS = 2
SUB = 8

forget_rate = 0.98
precise = lax.Precision.HIGHEST
three = lax.Precision.HIGH
MIB = 1024 * 1024


def dot(a, b, contract, precision):
    return lax.dot_general(
        a, b, ((contract[0], contract[1]), ((), ())), precision=precision, preferred_element_type=jnp.float32
    )


def block_inverse(p):
    m = len(p)
    if m == 1:
        return [[1.0 / p[0][0]]]
    if m == 2:
        a, b, d = p[0][0], p[0][1], p[1][1]
        r = 1.0 / (a * d - b * b)
        return [[d * r, -b * r], [-b * r, a * r]]
    h = m // 2
    top = [[p[i][j] for j in range(h)] for i in range(h)]
    side = [[p[i][h + j] for j in range(h)] for i in range(h)]
    ti = block_inverse(top)
    ts = [[sum(ti[i][k] * side[k][j] for k in range(h)) for j in range(h)] for i in range(h)]
    schur = [[None] * h for _ in range(h)]
    for i in range(h):
        for j in range(i, h):
            schur[i][j] = p[h + i][h + j] - sum(side[k][i] * ts[k][j] for k in range(h))
            schur[j][i] = schur[i][j]
    si = block_inverse(schur)
    tss = [[sum(ts[i][k] * si[k][j] for k in range(h)) for j in range(h)] for i in range(h)]
    out = [[None] * m for _ in range(m)]
    for i in range(h):
        for j in range(h):
            out[i][h + j] = -tss[i][j]
            out[h + j][i] = -tss[i][j]
            out[h + i][h + j] = si[i][j]
            if j >= i:
                out[i][j] = ti[i][j] + sum(tss[i][k] * ts[j][k] for k in range(h))
                out[j][i] = out[i][j]
    return out


def total(values):
    values = list(values)
    while len(values) > 1:
        values = [values[i] + values[i + 1] if i + 1 < len(values) else values[i] for i in range(0, len(values), 2)]
    return values[0]


def sweep_inverse(tiles):
    n = tiles[0].shape[1]
    full = (SUB, n)
    lane = lax.broadcasted_iota(jnp.int32, (1, n), 1)
    sub = lax.broadcasted_iota(jnp.int32, (SUB, 1), 0)
    for t in range(n // SUB):
        k = t * SUB
        inside = (lane >= k) & (lane < k + SUB)
        rows = [tiles[t][u : u + 1, :] for u in range(SUB)]
        cols = [[jnp.broadcast_to(x[:, k + u : k + u + 1], full) for u in range(SUB)] for x in tiles]
        piv = [[cols[t][v][u : u + 1, :] for v in range(SUB)] for u in range(SUB)]
        inv = block_inverse(piv)
        rows = [jnp.where(inside, (lane == k + u).astype(jnp.float32), rows[u]) for u in range(SUB)]
        w = [total(inv[u][v] * rows[v] for v in range(SUB)) for u in range(SUB)]
        new = []
        for i, x in enumerate(tiles):
            if i == t:
                y = jnp.broadcast_to(w[0], full)
                for u in range(1, SUB):
                    y = jnp.where(sub == u, w[u], y)
            else:
                y = jnp.where(inside, 0.0, x) - total(cols[i][u] * w[u] for u in range(SUB))
            new.append(y)
        tiles = new
    return tiles


def split(x):
    high = x.astype(jnp.bfloat16)
    return high, (x - high.astype(jnp.float32)).astype(jnp.bfloat16)


def dot3(a, b, contract=((1,), (0,))):
    a_high, a_low = split(a)
    b_high, b_low = split(b)

    def one(x, y):
        return lax.dot_general(x, y, (contract, ((), ())), preferred_element_type=jnp.float32)

    return one(a_high, b_high) + (one(a_high, b_low) + one(a_low, b_high))


def exact(a, b, contract=((1,), (0,))):
    return lax.dot_general(a, b, (contract, ((), ())), precision=precise, preferred_element_type=jnp.float32)


def whole():
    return pl.BlockSpec(memory_space=pltpu.VMEM)


def scalar():
    return pl.BlockSpec(memory_space=pltpu.SMEM)


def params(mib):
    return pltpu.CompilerParams(vmem_limit_bytes=int(mib * MIB))


def f32(*shape):
    return jax.ShapeDtypeStruct(shape, jnp.float32)


def hot(values, count):
    return (lax.broadcasted_iota(jnp.int32, (count, values.shape[1]), 0) == values).astype(jnp.float32)


def vectors_of(kinds, readout):
    extra = 2 * SUB - readout.shape[0]
    table = jnp.concatenate([readout, jnp.zeros((extra, readout.shape[1]), jnp.float32)], axis=0)
    which = hot(kinds, 2 * SUB).astype(jnp.bfloat16)
    out = 0.0
    for _ in range(3):
        part = table.astype(jnp.bfloat16)
        table = table - part.astype(jnp.float32)
        out = out + lax.dot_general(which, part, (((0,), (0,)), ((), ())), preferred_element_type=jnp.float32)
    return out


def layer(atoms, weights, bias, vectors):
    hidden = jnp.tanh(dot3(atoms, weights) + bias)
    return hidden * vectors, (1.0 - hidden * hidden) * vectors


def first_kernel(
    atoms_ref, next_ref, kinds_ref, member_ref, weights_ref, bias_ref, readout_ref, out_ref, packed_ref, turned, masked
):
    local = next_ref.shape[0]
    lines = local // FEATURES
    packed_ref[:local, :] = next_ref[...]
    packed_ref[local:, :] = jnp.zeros((packed_ref.shape[0] - local, FEATURES), jnp.float32)
    for which, ref in enumerate((kinds_ref, member_ref)):
        for u in range(lines):
            values = ref[1:2, u * FEATURES : (u + 1) * FEATURES].astype(jnp.float32)
            place = local + which * lines + u
            packed_ref[place : place + 1, :] = values
    atoms = atoms_ref[...]
    vectors = vectors_of(kinds_ref[0:1, :], readout_ref[...])
    energy, slope = layer(atoms, weights_ref[...], bias_ref[...], vectors)
    group_hot = hot(member_ref[0:1, :], GROUP_LOCAL)
    turned[...] = atoms.T
    for i in range(FEATURES):
        masked[SUB * i : SUB * i + SUB, :] = turned[i : i + 1, :] * group_hot
    grads = dot3(masked[...], slope)
    energies = jnp.sum(dot3(group_hot, energy), axis=1, keepdims=True)
    energies = jnp.broadcast_to(energies, (GROUP_LOCAL, FEATURES))
    blocks, _, wide = out_ref.shape
    per = FEATURES // blocks
    for j in range(blocks):
        for f in range(per):
            i = j * per + f
            out_ref[j, :, f * FEATURES : (f + 1) * FEATURES] = grads[SUB * i : SUB * i + SUB]
        out_ref[j, :, wide - FEATURES :] = energies


def first_terms(atoms, kinds, member, weights, bias, readout, cols, width):
    local = atoms.shape[1]
    return pl.pallas_call(
        first_kernel,
        grid=(1,),
        out_shape=(f32(cols, GROUP_LOCAL, width + FEATURES), f32(local + SUB, FEATURES)),
        in_specs=[
            pl.BlockSpec((None, local, FEATURES), lambda n: (0, 0, 0)),
            pl.BlockSpec((None, local, FEATURES), lambda n: (1, 0, 0)),
        ]
        + [whole()] * 5,
        out_specs=(whole(), whole()),
        scratch_shapes=[pltpu.VMEM((FEATURES, local), jnp.float32), pltpu.VMEM((SUB * FEATURES, local), jnp.float32)],
        compiler_params=params(63.9),
        name="first_terms",
    )(atoms, atoms, kinds, member, weights, bias, readout)


def prepare_kernel(col_ref, gathered_ref, readout_ref, atoms_ref, vectors_ref, masked_ref, turned):
    blocks = gathered_ref.shape[0]
    local = vectors_ref.shape[0] // blocks
    lines = local // FEATURES
    high_rows = (masked_ref.shape[0] - 2 * SUB) // 2
    count = high_rows // GROUP_LOCAL
    first = pl.multiple_of(col_ref[0] * count, SUB)
    for block in range(blocks):

        def row(start):
            parts = [gathered_ref[block, start + u : start + u + 1, :] for u in range(lines)]
            return jnp.concatenate(parts, axis=1).astype(jnp.int32)

        here = slice(block * local, (block + 1) * local)
        vectors_ref[here, :] = vectors_of(row(local), readout_ref[...])
        group_hot = hot(row(local + lines), GROUP_LOCAL)
        atoms = gathered_ref[block, :local, :]
        high, low = split(atoms)
        atoms_ref[here, :FEATURES] = high
        atoms_ref[here, FEATURES:] = low
        turned[block] = atoms.T
        part = turned[block, pl.ds(first, count), :]
        high, low = split(jnp.concatenate([part[f : f + 1, :] * group_hot for f in range(count)], axis=0))
        masked_ref[:high_rows, here] = high
        masked_ref[high_rows : 2 * high_rows, here] = low
        pair = jnp.concatenate([group_hot, jnp.zeros_like(group_hot)], axis=0)
        masked_ref[2 * high_rows :, here] = pair.astype(jnp.bfloat16)


def bf16(*shape):
    return jax.ShapeDtypeStruct(shape, jnp.bfloat16)


def prepare(gathered, readout, col_index, local, count):
    cols, tall, _ = gathered.shape
    lines = 2 * GROUP_LOCAL * (count + 1)
    parts = 4
    each = cols // parts
    return pl.pallas_call(
        prepare_kernel,
        grid=(parts,),
        out_shape=(bf16(cols * local, 2 * FEATURES), f32(cols * local, FEATURES), bf16(lines, cols * local)),
        in_specs=[scalar(), pl.BlockSpec((each, tall, FEATURES), lambda n: (n, 0, 0)), whole()],
        out_specs=(
            pl.BlockSpec((each * local, 2 * FEATURES), lambda n: (n, 0)),
            pl.BlockSpec((each * local, FEATURES), lambda n: (n, 0)),
            pl.BlockSpec((lines, each * local), lambda n: (0, n)),
        ),
        scratch_shapes=[pltpu.VMEM((each, FEATURES, local), jnp.float32)],
        compiler_params=params(63),
        name="prepare_terms",
    )(col_index, gathered, readout)


def later_kernel(atoms_ref, vectors_ref, masked_ref, weights_ref, bias_ref, out_ref, acc):
    step = pl.program_id(0)
    rows = masked_ref.shape[0] - 2 * SUB
    w_high, w_low = split(weights_ref[...])
    table = jnp.concatenate(
        [jnp.concatenate([w_high, w_low], axis=1), jnp.concatenate([w_high, jnp.zeros_like(w_low)], axis=1)], axis=0
    )
    preact = jnp.dot(atoms_ref[...], table, preferred_element_type=jnp.float32)
    hidden = jnp.tanh(preact[:, :FEATURES] + preact[:, FEATURES:] + bias_ref[...])
    vectors = vectors_ref[...]
    slope = jnp.concatenate(split((1.0 - hidden * hidden) * vectors), axis=1)
    energy = jnp.concatenate(split(hidden * vectors), axis=1)
    grads = jnp.dot(masked_ref[:rows, :], slope, preferred_element_type=jnp.float32)
    energies = jnp.dot(masked_ref[rows:, :], energy, preferred_element_type=jnp.float32)

    @pl.when(step == 0)
    def _():
        acc[:rows, :] = grads
        acc[rows:, :] = energies

    @pl.when(step > 0)
    def _():
        acc[:rows, :] += grads
        acc[rows:, :] += energies

    @pl.when(step == pl.num_programs(0) - 1)
    def _():
        both = acc[:, :FEATURES] + acc[:, FEATURES:]
        high_rows = rows // 2
        grads = both[:high_rows] + both[high_rows:rows]
        for f in range(high_rows // SUB):
            out_ref[:, f * FEATURES : (f + 1) * FEATURES] = grads[SUB * f : SUB * f + SUB]
        total_energy = jnp.sum(both[rows : rows + SUB], axis=1, keepdims=True)
        out_ref[:, high_rows // SUB * FEATURES :] = jnp.broadcast_to(total_energy, (GROUP_LOCAL, FEATURES))


def later_terms(terms, weights, bias):
    atoms, vectors, masked = terms
    parts = 4
    lines, count = masked.shape
    width = (lines // (2 * GROUP_LOCAL) - 1) * FEATURES
    each = count // parts
    return pl.pallas_call(
        later_kernel,
        grid=(parts,),
        out_shape=f32(GROUP_LOCAL, width + FEATURES),
        in_specs=[
            pl.BlockSpec((each, 2 * FEATURES), lambda n: (n, 0)),
            pl.BlockSpec((each, FEATURES), lambda n: (n, 0)),
            pl.BlockSpec((lines, each), lambda n: (0, n)),
            whole(),
            whole(),
        ],
        out_specs=whole(),
        scratch_shapes=[pltpu.VMEM((lines, 2 * FEATURES), jnp.float32)],
        compiler_params=params(63),
        name="later_terms",
    )(atoms, vectors, masked, weights, bias)


def downdate_kernel(cov_ref, first_ref, second_ref, scaled_ref, inverse_ref, gains_ref, out_ref, high, low):
    groups = scaled_ref.shape[0]

    @pl.when(pl.program_id(0) == 0)
    def _():
        fresh = dot3(inverse_ref[...], gains_ref[...]) * (1.0 / forget_rate)
        for place, value in ((0, scaled_ref[...] * (1.0 / forget_rate**2)), (groups, fresh)):
            value_high, value_low = split(value)
            high[place : place + groups, :] = value_high
            low[place : place + groups, :] = value_low

    def rows(ref):
        return ref[:, :GROUP_LOCAL, :].reshape(groups, ref.shape[2])

    left_high, left_low = split(jnp.concatenate([rows(first_ref), rows(second_ref)], axis=0).T)

    def one(x, y):
        return jnp.dot(x, y[...], preferred_element_type=jnp.float32)

    change = one(left_high, high) + (one(left_high, low) + one(left_low, high))
    out_ref[...] = cov_ref[...] * (1.0 / forget_rate**2) - change


def downdate(cov, first, second, scaled, inverse, gains):
    rows, width = cov.shape
    part = 256
    cols, tall, _ = first.shape
    block = pl.BlockSpec((cols, tall, part), lambda n: (0, 0, n))
    return pl.pallas_call(
        downdate_kernel,
        grid=(rows // part,),
        out_shape=f32(rows, width),
        in_specs=[pl.BlockSpec((part, width), lambda n: (n, 0)), block, block, whole(), whole(), whole()],
        out_specs=pl.BlockSpec((part, width), lambda n: (n, 0)),
        scratch_shapes=[pltpu.VMEM((2 * scaled.shape[0], width), jnp.bfloat16)] * 2,
        compiler_params=params(60.1),
        name="downdate",
    )(cov, first, second, scaled, inverse, gains)


def pack_kernel(parts_ref, gains_ref, out_ref):
    width = gains_ref.shape[1]
    part = total(parts_ref[i] for i in range(parts_ref.shape[0]))
    for copy in range(out_ref.shape[0]):
        out_ref[copy, :, :width] = gains_ref[...]
        out_ref[copy, :, width:] = part


def pack(parts, gains, copies):
    sub, width = gains.shape
    return pl.pallas_call(
        pack_kernel,
        out_shape=f32(copies, sub, width + parts.shape[2]),
        in_specs=[whole(), whole()],
        out_specs=whole(),
        compiler_params=params(8),
        name="pack_gains",
    )(parts, gains)


def update_kernel(order, side_ref, own_ref, other_ref, energy_ref, targets_ref, inverse_ref, gains_ref, change_ref, both):
    n = targets_ref.shape[0]
    width = own_ref.shape[2] - n
    half = own_ref.shape[0]
    side = side_ref[0]
    both[pl.ds(side * half, half)] = own_ref[...]
    both[pl.ds((1 - side) * half, half)] = other_ref[...]
    places = [order.index(t) for t in range(n // SUB)]
    curvature = jnp.concatenate([both[p, :, width:] for p in places], axis=0)
    row = lax.broadcasted_iota(jnp.int32, (n, n), 0)
    col = lax.broadcasted_iota(jnp.int32, (n, n), 1)
    innovation = 0.5 * (curvature + curvature.T) + jnp.where(row == col, forget_rate, 0.0)
    tiles = sweep_inverse([innovation[SUB * i : SUB * i + SUB] for i in range(n // SUB)])
    weighted = []
    for i, x in enumerate(tiles):
        here = slice(SUB * i, SUB * i + SUB)
        inverse_ref[here, :] = x
        weighted.append(x * (targets_ref[here, :] - energy_ref[here, :]))
    coefficient = jnp.broadcast_to(jnp.sum(total(weighted), axis=0, keepdims=True), (SUB, n))
    gains = jnp.concatenate([both[p, :, :width] for p in places], axis=0)
    gains_ref[...] = gains
    moved = exact(coefficient, gains)
    sub = lax.broadcasted_iota(jnp.int32, (SUB, FEATURES), 0)
    change = moved[:, :FEATURES]
    for r in range(1, width // FEATURES):
        change = jnp.where(sub == r, moved[:, r * FEATURES : (r + 1) * FEATURES], change)
    for j in range(change_ref.shape[0]):
        change_ref[j] = change


def solve_update(side, own, other, stacked, targets, copies, order):
    n = targets.shape[0]
    half, sub, wide = own.shape
    last = stacked.shape[1] // FEATURES - 1
    return pl.pallas_call(
        functools.partial(update_kernel, order),
        grid=(1,),
        out_shape=(f32(n, n), f32(n, wide - n), f32(copies, SUB, FEATURES)),
        in_specs=[scalar(), whole(), whole(), pl.BlockSpec((n, FEATURES), lambda i: (0, last)), whole()],
        out_specs=(whole(), whole(), whole()),
        scratch_shapes=[pltpu.VMEM((2 * half, sub, wide), jnp.float32)],
        compiler_params=params(8),
        name="inverse_and_change",
    )(side, own, other, stacked, targets)


def exchange(chunks, axis):
    return lax.all_to_all(chunks, axis, 0, 0, tiled=True)


def spread(x, axis):
    return exchange(jnp.broadcast_to(x[None], (lax.axis_size(axis),) + x.shape), axis)


def gather_pair(copies):
    count = copies.shape[0]
    lanes = [[core + 2 * z for z in range(count)] for core in range(2)]
    own = lax.all_to_all(copies, "grp", 0, 0, tiled=True, axis_index_groups=lanes)
    other = lax.ppermute(own, "grp", [(i, i ^ 1) for i in range(2 * count)])
    return own, other


def far_row(j, side):
    return (j // side + side // 2) % side * side + (j % side + side // 2) % side


def swap(x, chunk_of_row):
    size = len(chunk_of_row)
    pairs = [(i * size + chunk_of_row[a], a * size + i) for i in range(size) for a in range(size)]
    return lax.ppermute(x, ("grp", "atm"), pairs)


def gather_rows(own):
    twice = jnp.concatenate([own, own], axis=0)
    return lax.all_gather(twice, "atm", axis=0, tiled=False)


def together(*values):
    return lax.optimization_barrier(values)


def body(atoms, kinds, member, targets, weights, bias, readout, covariance):
    rows, cols = lax.axis_size("grp"), lax.axis_size("atm")
    chips = rows // 2
    col_index = lax.axis_index("atm").reshape(1)
    side = (lax.axis_index("grp") % 2).reshape(1)
    local = atoms.shape[1]
    groups = GROUP_LOCAL * rows
    width = covariance.shape[1]
    bias = bias.reshape(1, FEATURES)
    ordered = jnp.broadcast_to(targets[:, :, None], (STEPS, groups, FEATURES))
    chunk_of_row = [far_row(a, math.isqrt(rows)) for a in range(rows)]
    order = [chunk_of_row[2 * z + core] for core in range(2) for z in range(chips)]
    current = weights
    row_gains = []
    for step in range(STEPS):
        if step == 0:
            chunks, packed = first_terms(atoms, kinds, member, current, bias, readout, cols, width)
            gathered = lax.all_gather(packed, "atm", axis=0, tiled=False)
            chunk = exchange(chunks, "atm").sum(axis=0)
        else:
            chunk = later_terms(later, current, bias)
        stacked = lax.all_gather(chunk, "grp", axis=0, tiled=True)
        jac = stacked[:, :width]
        terms = dot(jac, covariance, ((1,), (1,)), three)
        if step:
            moved = dot(jac, scaled, ((1,), (1,)), three)
            gains = row_gains[0][:, :GROUP_LOCAL].reshape(groups, width)
            terms = (terms - dot(moved, gains, ((1,), (0,)), three)) / forget_rate
        own = exchange(terms.reshape(cols, groups // cols, width), "atm").sum(axis=0)
        if step == 0:
            own, gathered, ordered = together(own, gathered, ordered)
        row_gains.append(gather_rows(own))
        other = swap(own, chunk_of_row)
        if step == 0:
            later = prepare(gathered, readout, col_index, local, width // FEATURES)
            other, *later = together(other, *later)
        part = spread(dot(other, jac, ((1,), (1,)), precise), "atm")
        got_own, got_other = gather_pair(pack(part, other, chips))
        inverse, col_gains, change = solve_update(
            side, got_own, got_other, stacked, ordered[step], cols, order
        )
        if step == STEPS - 1:
            change, *row_gains = together(change, *row_gains)
        change = exchange(change, "atm")
        current = current + change.reshape(FEATURES, FEATURES)
        if step == 0:
            scaled = dot(inverse, col_gains, ((1,), (0,)), precise)
    covar = downdate(covariance, *row_gains, scaled, inverse, col_gains)
    return (covar, current)


def solution(mesh):
    return jax.shard_map(
        body,
        mesh=mesh,
        in_specs=(
            P(None, ("grp", "atm"), None),
            P(None, ("grp", "atm")),
            P(None, ("grp", "atm")),
            P(),
            P(),
            P(),
            P(),
            P("grp", "atm"),
        ),
        out_specs=(P("grp", "atm"), P()),
        check_vma=False,
    )
```

```python
import functools
import math

import jax
import jax.numpy as jnp
from jax import lax
from jax.experimental import pallas as pl
from jax.experimental.pallas import tpu as pltpu
from jax.sharding import PartitionSpec as P

FEATURES = 128
GROUP_LOCAL = 8
STEPS = 2
SUB = 8

forget_rate = 0.98
precise = lax.Precision.HIGHEST
three = lax.Precision.HIGH
MIB = 1024 * 1024


def dot(a, b, contract, precision):
    return lax.dot_general(
        a, b, ((contract[0], contract[1]), ((), ())), precision=precision, preferred_element_type=jnp.float32
    )


def block_inverse(p):
    m = len(p)
    if m == 1:
        return [[1.0 / p[0][0]]]
    if m == 2:
        a, b, d = p[0][0], p[0][1], p[1][1]
        r = 1.0 / (a * d - b * b)
        return [[d * r, -b * r], [-b * r, a * r]]
    h = m // 2
    top = [[p[i][j] for j in range(h)] for i in range(h)]
    side = [[p[i][h + j] for j in range(h)] for i in range(h)]
    ti = block_inverse(top)
    ts = [[sum(ti[i][k] * side[k][j] for k in range(h)) for j in range(h)] for i in range(h)]
    schur = [[None] * h for _ in range(h)]
    for i in range(h):
        for j in range(i, h):
            schur[i][j] = p[h + i][h + j] - sum(side[k][i] * ts[k][j] for k in range(h))
            schur[j][i] = schur[i][j]
    si = block_inverse(schur)
    tss = [[sum(ts[i][k] * si[k][j] for k in range(h)) for j in range(h)] for i in range(h)]
    out = [[None] * m for _ in range(m)]
    for i in range(h):
        for j in range(h):
            out[i][h + j] = -tss[i][j]
            out[h + j][i] = -tss[i][j]
            out[h + i][h + j] = si[i][j]
            if j >= i:
                out[i][j] = ti[i][j] + sum(tss[i][k] * ts[j][k] for k in range(h))
                out[j][i] = out[i][j]
    return out


def total(values):
    values = list(values)
    while len(values) > 1:
        values = [values[i] + values[i + 1] if i + 1 < len(values) else values[i] for i in range(0, len(values), 2)]
    return values[0]


def sweep_inverse(tiles):
    n = tiles[0].shape[1]
    full = (SUB, n)
    lane = lax.broadcasted_iota(jnp.int32, (1, n), 1)
    sub = lax.broadcasted_iota(jnp.int32, (SUB, 1), 0)
    for t in range(n // SUB):
        k = t * SUB
        inside = (lane >= k) & (lane < k + SUB)
        rows = [tiles[t][u : u + 1, :] for u in range(SUB)]
        cols = [[jnp.broadcast_to(x[:, k + u : k + u + 1], full) for u in range(SUB)] for x in tiles]
        piv = [[cols[t][v][u : u + 1, :] for v in range(SUB)] for u in range(SUB)]
        inv = block_inverse(piv)
        rows = [jnp.where(inside, (lane == k + u).astype(jnp.float32), rows[u]) for u in range(SUB)]
        w = [total(inv[u][v] * rows[v] for v in range(SUB)) for u in range(SUB)]
        new = []
        for i, x in enumerate(tiles):
            if i == t:
                y = jnp.broadcast_to(w[0], full)
                for u in range(1, SUB):
                    y = jnp.where(sub == u, w[u], y)
            else:
                y = jnp.where(inside, 0.0, x) - total(cols[i][u] * w[u] for u in range(SUB))
            new.append(y)
        tiles = new
    return tiles


def split(x):
    high = x.astype(jnp.bfloat16)
    return high, (x - high.astype(jnp.float32)).astype(jnp.bfloat16)


def dot3(a, b, contract=((1,), (0,))):
    a_high, a_low = split(a)
    b_high, b_low = split(b)

    def one(x, y):
        return lax.dot_general(x, y, (contract, ((), ())), preferred_element_type=jnp.float32)

    return one(a_high, b_high) + (one(a_high, b_low) + one(a_low, b_high))


def exact(a, b, contract=((1,), (0,))):
    return lax.dot_general(a, b, (contract, ((), ())), precision=precise, preferred_element_type=jnp.float32)


def whole():
    return pl.BlockSpec(memory_space=pltpu.VMEM)


def scalar():
    return pl.BlockSpec(memory_space=pltpu.SMEM)


def params(mib):
    return pltpu.CompilerParams(vmem_limit_bytes=int(mib * MIB))


def f32(*shape):
    return jax.ShapeDtypeStruct(shape, jnp.float32)


def hot(values, count):
    return (lax.broadcasted_iota(jnp.int32, (count, values.shape[1]), 0) == values).astype(jnp.float32)


def vectors_of(kinds, readout):
    extra = 2 * SUB - readout.shape[0]
    table = jnp.concatenate([readout, jnp.zeros((extra, readout.shape[1]), jnp.float32)], axis=0)
    which = hot(kinds, 2 * SUB).astype(jnp.bfloat16)
    out = 0.0
    for _ in range(3):
        part = table.astype(jnp.bfloat16)
        table = table - part.astype(jnp.float32)
        out = out + lax.dot_general(which, part, (((0,), (0,)), ((), ())), preferred_element_type=jnp.float32)
    return out


def layer(atoms, weights, bias, vectors):
    hidden = jnp.tanh(dot3(atoms, weights) + bias)
    return hidden * vectors, (1.0 - hidden * hidden) * vectors


def first_kernel(
    atoms_ref, next_ref, kinds_ref, member_ref, weights_ref, bias_ref, readout_ref, out_ref, packed_ref, turned, masked
):
    local = next_ref.shape[0]
    lines = local // FEATURES
    packed_ref[:local, :] = next_ref[...]
    packed_ref[local:, :] = jnp.zeros((packed_ref.shape[0] - local, FEATURES), jnp.float32)
    for which, ref in enumerate((kinds_ref, member_ref)):
        for u in range(lines):
            values = ref[1:2, u * FEATURES : (u + 1) * FEATURES].astype(jnp.float32)
            place = local + which * lines + u
            packed_ref[place : place + 1, :] = values
    atoms = atoms_ref[...]
    vectors = vectors_of(kinds_ref[0:1, :], readout_ref[...])
    energy, slope = layer(atoms, weights_ref[...], bias_ref[...], vectors)
    group_hot = hot(member_ref[0:1, :], GROUP_LOCAL)
    turned[...] = atoms.T
    for i in range(FEATURES):
        masked[SUB * i : SUB * i + SUB, :] = turned[i : i + 1, :] * group_hot
    grads = dot3(masked[...], slope)
    energies = jnp.sum(dot3(group_hot, energy), axis=1, keepdims=True)
    energies = jnp.broadcast_to(energies, (GROUP_LOCAL, FEATURES))
    blocks, _, wide = out_ref.shape
    per = FEATURES // blocks
    for j in range(blocks):
        for f in range(per):
            i = j * per + f
            out_ref[j, :, f * FEATURES : (f + 1) * FEATURES] = grads[SUB * i : SUB * i + SUB]
        out_ref[j, :, wide - FEATURES :] = energies


def first_terms(atoms, kinds, member, weights, bias, readout, cols, width):
    local = atoms.shape[1]
    return pl.pallas_call(
        first_kernel,
        grid=(1,),
        out_shape=(f32(cols, GROUP_LOCAL, width + FEATURES), f32(local + SUB, FEATURES)),
        in_specs=[
            pl.BlockSpec((None, local, FEATURES), lambda n: (0, 0, 0)),
            pl.BlockSpec((None, local, FEATURES), lambda n: (1, 0, 0)),
        ]
        + [whole()] * 5,
        out_specs=(whole(), whole()),
        scratch_shapes=[pltpu.VMEM((FEATURES, local), jnp.float32), pltpu.VMEM((SUB * FEATURES, local), jnp.float32)],
        compiler_params=params(63.9),
        name="first_terms",
    )(atoms, atoms, kinds, member, weights, bias, readout)


def prepare_kernel(col_ref, gathered_ref, readout_ref, atoms_ref, vectors_ref, masked_ref, turned):
    blocks = gathered_ref.shape[0]
    local = vectors_ref.shape[0] // blocks
    lines = local // FEATURES
    high_rows = (masked_ref.shape[0] - 2 * SUB) // 2
    count = high_rows // GROUP_LOCAL
    first = pl.multiple_of(col_ref[0] * count, SUB)
    for block in range(blocks):

        def row(start):
            parts = [gathered_ref[block, start + u : start + u + 1, :] for u in range(lines)]
            return jnp.concatenate(parts, axis=1).astype(jnp.int32)

        here = slice(block * local, (block + 1) * local)
        vectors_ref[here, :] = vectors_of(row(local), readout_ref[...])
        group_hot = hot(row(local + lines), GROUP_LOCAL)
        atoms = gathered_ref[block, :local, :]
        high, low = split(atoms)
        atoms_ref[here, :FEATURES] = high
        atoms_ref[here, FEATURES:] = low
        turned[block] = atoms.T
        part = turned[block, pl.ds(first, count), :]
        high, low = split(jnp.concatenate([part[f : f + 1, :] * group_hot for f in range(count)], axis=0))
        masked_ref[:high_rows, here] = high
        masked_ref[high_rows : 2 * high_rows, here] = low
        pair = jnp.concatenate([group_hot, jnp.zeros_like(group_hot)], axis=0)
        masked_ref[2 * high_rows :, here] = pair.astype(jnp.bfloat16)


def bf16(*shape):
    return jax.ShapeDtypeStruct(shape, jnp.bfloat16)


def prepare(gathered, readout, col_index, local, count):
    cols, tall, _ = gathered.shape
    lines = 2 * GROUP_LOCAL * (count + 1)
    parts = 4
    each = cols // parts
    return pl.pallas_call(
        prepare_kernel,
        grid=(parts,),
        out_shape=(bf16(cols * local, 2 * FEATURES), f32(cols * local, FEATURES), bf16(lines, cols * local)),
        in_specs=[scalar(), pl.BlockSpec((each, tall, FEATURES), lambda n: (n, 0, 0)), whole()],
        out_specs=(
            pl.BlockSpec((each * local, 2 * FEATURES), lambda n: (n, 0)),
            pl.BlockSpec((each * local, FEATURES), lambda n: (n, 0)),
            pl.BlockSpec((lines, each * local), lambda n: (0, n)),
        ),
        scratch_shapes=[pltpu.VMEM((each, FEATURES, local), jnp.float32)],
        compiler_params=params(63),
        name="prepare_terms",
    )(col_index, gathered, readout)


def later_kernel(atoms_ref, vectors_ref, masked_ref, weights_ref, bias_ref, out_ref, acc):
    step = pl.program_id(0)
    rows = masked_ref.shape[0] - 2 * SUB
    w_high, w_low = split(weights_ref[...])
    table = jnp.concatenate(
        [jnp.concatenate([w_high, w_low], axis=1), jnp.concatenate([w_high, jnp.zeros_like(w_low)], axis=1)], axis=0
    )
    preact = jnp.dot(atoms_ref[...], table, preferred_element_type=jnp.float32)
    hidden = jnp.tanh(preact[:, :FEATURES] + preact[:, FEATURES:] + bias_ref[...])
    vectors = vectors_ref[...]
    slope = jnp.concatenate(split((1.0 - hidden * hidden) * vectors), axis=1)
    energy = jnp.concatenate(split(hidden * vectors), axis=1)
    grads = jnp.dot(masked_ref[:rows, :], slope, preferred_element_type=jnp.float32)
    energies = jnp.dot(masked_ref[rows:, :], energy, preferred_element_type=jnp.float32)

    @pl.when(step == 0)
    def _():
        acc[:rows, :] = grads
        acc[rows:, :] = energies

    @pl.when(step > 0)
    def _():
        acc[:rows, :] += grads
        acc[rows:, :] += energies

    @pl.when(step == pl.num_programs(0) - 1)
    def _():
        both = acc[:, :FEATURES] + acc[:, FEATURES:]
        high_rows = rows // 2
        grads = both[:high_rows] + both[high_rows:rows]
        for f in range(high_rows // SUB):
            out_ref[:, f * FEATURES : (f + 1) * FEATURES] = grads[SUB * f : SUB * f + SUB]
        total_energy = jnp.sum(both[rows : rows + SUB], axis=1, keepdims=True)
        out_ref[:, high_rows // SUB * FEATURES :] = jnp.broadcast_to(total_energy, (GROUP_LOCAL, FEATURES))


def later_terms(terms, weights, bias):
    atoms, vectors, masked = terms
    parts = 4
    lines, count = masked.shape
    width = (lines // (2 * GROUP_LOCAL) - 1) * FEATURES
    each = count // parts
    return pl.pallas_call(
        later_kernel,
        grid=(parts,),
        out_shape=f32(GROUP_LOCAL, width + FEATURES),
        in_specs=[
            pl.BlockSpec((each, 2 * FEATURES), lambda n: (n, 0)),
            pl.BlockSpec((each, FEATURES), lambda n: (n, 0)),
            pl.BlockSpec((lines, each), lambda n: (0, n)),
            whole(),
            whole(),
        ],
        out_specs=whole(),
        scratch_shapes=[pltpu.VMEM((lines, 2 * FEATURES), jnp.float32)],
        compiler_params=params(63),
        name="later_terms",
    )(atoms, vectors, masked, weights, bias)


def downdate_kernel(scale, fresh, cov_ref, rows_ref, *rest):
    out_ref, table = rest[-2:]
    groups = table.shape[0] // 3

    @pl.when(pl.program_id(0) == 0)
    def _():
        if fresh:
            right = dot3(rest[0][...], rest[1][...]) * (1.0 / forget_rate)
        else:
            right = rest[0][...] * (1.0 / forget_rate**2)
        high, low = split(right)
        table[:groups, :] = high
        table[groups : 2 * groups, :] = high
        table[2 * groups :, :] = low

    left = rows_ref[:, :GROUP_LOCAL, :].reshape(groups, rows_ref.shape[2]).T
    high, low = split(left)
    change = jnp.dot(jnp.concatenate([high, low], axis=1), table[: 2 * groups, :], preferred_element_type=jnp.float32)
    change = change + jnp.dot(high, table[2 * groups :, :], preferred_element_type=jnp.float32)
    cov = cov_ref[...]
    out_ref[...] = (cov * scale if scale != 1.0 else cov) - change


def downdate(cov, gathered_rows, right, scale):
    rows, width = cov.shape
    part = 256
    cols, tall, _ = gathered_rows.shape
    return pl.pallas_call(
        functools.partial(downdate_kernel, scale, len(right) == 2),
        grid=(rows // part,),
        out_shape=f32(rows, width),
        in_specs=[
            pl.BlockSpec((part, width), lambda n: (n, 0)),
            pl.BlockSpec((cols, tall, part), lambda n: (0, 0, n)),
        ]
        + [whole()] * len(right),
        out_specs=pl.BlockSpec((part, width), lambda n: (n, 0)),
        scratch_shapes=[pltpu.VMEM((3 * GROUP_LOCAL * cols, width), jnp.bfloat16)],
        compiler_params=params(16 if len(right) == 2 else 60.1),
        name="downdate",
    )(cov, gathered_rows, *right)


def pack_kernel(parts_ref, gains_ref, out_ref):
    width = gains_ref.shape[1]
    part = total(parts_ref[i] for i in range(parts_ref.shape[0]))
    for copy in range(out_ref.shape[0]):
        out_ref[copy, :, :width] = gains_ref[...]
        out_ref[copy, :, width:] = part


def pack(parts, gains, copies):
    sub, width = gains.shape
    return pl.pallas_call(
        pack_kernel,
        out_shape=f32(copies, sub, width + parts.shape[2]),
        in_specs=[whole(), whole()],
        out_specs=whole(),
        compiler_params=params(8),
        name="pack_gains",
    )(parts, gains)


def update_kernel(order, side_ref, own_ref, other_ref, energy_ref, targets_ref, inverse_ref, gains_ref, change_ref, both):
    n = targets_ref.shape[0]
    width = own_ref.shape[2] - n
    half = own_ref.shape[0]
    side = side_ref[0]
    both[pl.ds(side * half, half)] = own_ref[...]
    both[pl.ds((1 - side) * half, half)] = other_ref[...]
    places = [order.index(t) for t in range(n // SUB)]
    curvature = jnp.concatenate([both[p, :, width:] for p in places], axis=0)
    row = lax.broadcasted_iota(jnp.int32, (n, n), 0)
    col = lax.broadcasted_iota(jnp.int32, (n, n), 1)
    innovation = 0.5 * (curvature + curvature.T) + jnp.where(row == col, forget_rate, 0.0)
    tiles = sweep_inverse([innovation[SUB * i : SUB * i + SUB] for i in range(n // SUB)])
    weighted = []
    for i, x in enumerate(tiles):
        here = slice(SUB * i, SUB * i + SUB)
        inverse_ref[here, :] = x
        weighted.append(x * (targets_ref[here, :] - energy_ref[here, :]))
    coefficient = jnp.broadcast_to(jnp.sum(total(weighted), axis=0, keepdims=True), (SUB, n))
    gains = jnp.concatenate([both[p, :, :width] for p in places], axis=0)
    gains_ref[...] = gains
    moved = dot3(coefficient, gains)
    sub = lax.broadcasted_iota(jnp.int32, (SUB, FEATURES), 0)
    change = moved[:, :FEATURES]
    for r in range(1, width // FEATURES):
        change = jnp.where(sub == r, moved[:, r * FEATURES : (r + 1) * FEATURES], change)
    for j in range(change_ref.shape[0]):
        change_ref[j] = change


def solve_update(side, own, other, stacked, targets, copies, order):
    n = targets.shape[0]
    half, sub, wide = own.shape
    last = stacked.shape[1] // FEATURES - 1
    return pl.pallas_call(
        functools.partial(update_kernel, order),
        grid=(1,),
        out_shape=(f32(n, n), f32(n, wide - n), f32(copies, SUB, FEATURES)),
        in_specs=[scalar(), whole(), whole(), pl.BlockSpec((n, FEATURES), lambda i: (0, last)), whole()],
        out_specs=(whole(), whole(), whole()),
        scratch_shapes=[pltpu.VMEM((2 * half, sub, wide), jnp.float32)],
        compiler_params=params(8),
        name="inverse_and_change",
    )(side, own, other, stacked, targets)


def exchange(chunks, axis):
    return lax.all_to_all(chunks, axis, 0, 0, tiled=True)


def spread(x, axis):
    return exchange(jnp.broadcast_to(x[None], (lax.axis_size(axis),) + x.shape), axis)


def gather_pair(copies):
    count = copies.shape[0]
    lanes = [[core + 2 * z for z in range(count)] for core in range(2)]
    own = lax.all_to_all(copies, "grp", 0, 0, tiled=True, axis_index_groups=lanes)
    other = lax.ppermute(own, "grp", [(i, i ^ 1) for i in range(2 * count)])
    return own, other


def far_row(j, side):
    return (j // side + side // 2) % side * side + (j % side + side // 2) % side


def swap(x, chunk_of_row):
    size = len(chunk_of_row)
    pairs = [(i * size + chunk_of_row[a], a * size + i) for i in range(size) for a in range(size)]
    return lax.ppermute(x, ("grp", "atm"), pairs)


def gather_rows(own):
    twice = jnp.concatenate([own, own], axis=0)
    return lax.all_gather(twice, "atm", axis=0, tiled=False)


def together(*values):
    return lax.optimization_barrier(values)


def body(atoms, kinds, member, targets, weights, bias, readout, covariance):
    rows, cols = lax.axis_size("grp"), lax.axis_size("atm")
    chips = rows // 2
    col_index = lax.axis_index("atm").reshape(1)
    side = (lax.axis_index("grp") % 2).reshape(1)
    local = atoms.shape[1]
    groups = GROUP_LOCAL * rows
    width = covariance.shape[1]
    bias = bias.reshape(1, FEATURES)
    ordered = jnp.broadcast_to(targets[:, :, None], (STEPS, groups, FEATURES))
    chunk_of_row = [far_row(a, math.isqrt(rows)) for a in range(rows)]
    order = [chunk_of_row[2 * z + core] for core in range(2) for z in range(chips)]
    current = weights
    row_gains = []
    for step in range(STEPS):
        if step == 0:
            chunks, packed = first_terms(atoms, kinds, member, current, bias, readout, cols, width)
            gathered = lax.all_gather(packed, "atm", axis=0, tiled=False)
            chunk = exchange(chunks, "atm").sum(axis=0)
        else:
            chunk = later_terms(later, current, bias)
        stacked = lax.all_gather(chunk, "grp", axis=0, tiled=True)
        jac = stacked[:, :width]
        terms = dot(jac, covariance, ((1,), (1,)), three)
        if step:
            moved = dot(jac, scaled, ((1,), (1,)), three)
            gains = row_gains[0][:, :GROUP_LOCAL].reshape(groups, width)
            terms = (terms - dot(moved, gains, ((1,), (0,)), three)) / forget_rate
        own = exchange(terms.reshape(cols, groups // cols, width), "atm").sum(axis=0)
        if step:
            base = downdate(covariance, row_gains[0], (scaled,), 1.0 / forget_rate**2)
            own, base = together(own, base)
        else:
            own, gathered, ordered = together(own, gathered, ordered)
        row_gains.append(gather_rows(own))
        other = swap(own, chunk_of_row)
        if step == 0:
            later = prepare(gathered, readout, col_index, local, width // FEATURES)
            other, *later = together(other, *later)
        part = spread(dot(other, jac, ((1,), (1,)), precise), "atm")
        got_own, got_other = gather_pair(pack(part, other, chips))
        inverse, col_gains, change = solve_update(
            side, got_own, got_other, stacked, ordered[step], cols, order
        )
        if step == STEPS - 1:
            change, row_gains[1] = together(change, row_gains[1])
        change = exchange(change, "atm")
        current = current + change.reshape(FEATURES, FEATURES)
        if step == 0:
            scaled = dot(inverse, col_gains, ((1,), (0,)), precise)
    covar = downdate(base, row_gains[1], (inverse, col_gains), 1.0)
    return (covar, current)


def solution(mesh):
    return jax.shard_map(
        body,
        mesh=mesh,
        in_specs=(
            P(None, ("grp", "atm"), None),
            P(None, ("grp", "atm")),
            P(None, ("grp", "atm")),
            P(),
            P(),
            P(),
            P(),
            P("grp", "atm"),
        ),
        out_specs=(P("grp", "atm"), P()),
        check_vma=False,
    )
```

```python
import functools
import math

import jax
import jax.numpy as jnp
from jax import lax
from jax.experimental import pallas as pl
from jax.experimental.pallas import tpu as pltpu
from jax.sharding import PartitionSpec as P

FEATURES = 128
GROUP_LOCAL = 8
STEPS = 2
SUB = 8

forget_rate = 0.98
precise = lax.Precision.HIGHEST
three = lax.Precision.HIGH
MIB = 1024 * 1024


def dot(a, b, contract, precision):
    return lax.dot_general(
        a, b, ((contract[0], contract[1]), ((), ())), precision=precision, preferred_element_type=jnp.float32
    )


def block_inverse(p):
    m = len(p)
    if m == 1:
        return [[1.0 / p[0][0]]]
    if m == 2:
        a, b, d = p[0][0], p[0][1], p[1][1]
        r = 1.0 / (a * d - b * b)
        return [[d * r, -b * r], [-b * r, a * r]]
    h = m // 2
    top = [[p[i][j] for j in range(h)] for i in range(h)]
    side = [[p[i][h + j] for j in range(h)] for i in range(h)]
    ti = block_inverse(top)
    ts = [[sum(ti[i][k] * side[k][j] for k in range(h)) for j in range(h)] for i in range(h)]
    schur = [[None] * h for _ in range(h)]
    for i in range(h):
        for j in range(i, h):
            schur[i][j] = p[h + i][h + j] - sum(side[k][i] * ts[k][j] for k in range(h))
            schur[j][i] = schur[i][j]
    si = block_inverse(schur)
    tss = [[sum(ts[i][k] * si[k][j] for k in range(h)) for j in range(h)] for i in range(h)]
    out = [[None] * m for _ in range(m)]
    for i in range(h):
        for j in range(h):
            out[i][h + j] = -tss[i][j]
            out[h + j][i] = -tss[i][j]
            out[h + i][h + j] = si[i][j]
            if j >= i:
                out[i][j] = ti[i][j] + sum(tss[i][k] * ts[j][k] for k in range(h))
                out[j][i] = out[i][j]
    return out


def total(values):
    values = list(values)
    while len(values) > 1:
        values = [values[i] + values[i + 1] if i + 1 < len(values) else values[i] for i in range(0, len(values), 2)]
    return values[0]


def sweep_inverse(tiles):
    n = tiles[0].shape[1]
    full = (SUB, n)
    lane = lax.broadcasted_iota(jnp.int32, (1, n), 1)
    sub = lax.broadcasted_iota(jnp.int32, (SUB, 1), 0)
    for t in range(n // SUB):
        k = t * SUB
        inside = (lane >= k) & (lane < k + SUB)
        rows = [tiles[t][u : u + 1, :] for u in range(SUB)]
        cols = [[jnp.broadcast_to(x[:, k + u : k + u + 1], full) for u in range(SUB)] for x in tiles]
        piv = [[cols[t][v][u : u + 1, :] for v in range(SUB)] for u in range(SUB)]
        inv = block_inverse(piv)
        rows = [jnp.where(inside, (lane == k + u).astype(jnp.float32), rows[u]) for u in range(SUB)]
        w = [total(inv[u][v] * rows[v] for v in range(SUB)) for u in range(SUB)]
        new = []
        for i, x in enumerate(tiles):
            if i == t:
                y = jnp.broadcast_to(w[0], full)
                for u in range(1, SUB):
                    y = jnp.where(sub == u, w[u], y)
            else:
                y = jnp.where(inside, 0.0, x) - total(cols[i][u] * w[u] for u in range(SUB))
            new.append(y)
        tiles = new
    return tiles


def split(x):
    high = x.astype(jnp.bfloat16)
    return high, (x - high.astype(jnp.float32)).astype(jnp.bfloat16)


def dot3(a, b, contract=((1,), (0,))):
    a_high, a_low = split(a)
    b_high, b_low = split(b)

    def one(x, y):
        return lax.dot_general(x, y, (contract, ((), ())), preferred_element_type=jnp.float32)

    return one(a_high, b_high) + (one(a_high, b_low) + one(a_low, b_high))


def exact(a, b, contract=((1,), (0,))):
    return lax.dot_general(a, b, (contract, ((), ())), precision=precise, preferred_element_type=jnp.float32)


def whole():
    return pl.BlockSpec(memory_space=pltpu.VMEM)


def scalar():
    return pl.BlockSpec(memory_space=pltpu.SMEM)


def params(mib):
    return pltpu.CompilerParams(vmem_limit_bytes=int(mib * MIB))


def f32(*shape):
    return jax.ShapeDtypeStruct(shape, jnp.float32)


def hot(values, count):
    return (lax.broadcasted_iota(jnp.int32, (count, values.shape[1]), 0) == values).astype(jnp.float32)


def vectors_of(kinds, readout):
    extra = 2 * SUB - readout.shape[0]
    table = jnp.concatenate([readout, jnp.zeros((extra, readout.shape[1]), jnp.float32)], axis=0)
    which = hot(kinds, 2 * SUB).astype(jnp.bfloat16)
    out = 0.0
    for _ in range(3):
        part = table.astype(jnp.bfloat16)
        table = table - part.astype(jnp.float32)
        out = out + lax.dot_general(which, part, (((0,), (0,)), ((), ())), preferred_element_type=jnp.float32)
    return out


def layer(atoms, weights, bias, vectors):
    hidden = jnp.tanh(dot3(atoms, weights) + bias)
    return hidden * vectors, (1.0 - hidden * hidden) * vectors


def first_kernel(
    atoms_ref, next_ref, kinds_ref, member_ref, weights_ref, bias_ref, readout_ref, out_ref, packed_ref, turned, masked
):
    local = next_ref.shape[0]
    lines = local // FEATURES
    packed_ref[:local, :] = next_ref[...]
    packed_ref[local:, :] = jnp.zeros((packed_ref.shape[0] - local, FEATURES), jnp.float32)
    for which, ref in enumerate((kinds_ref, member_ref)):
        for u in range(lines):
            values = ref[1:2, u * FEATURES : (u + 1) * FEATURES].astype(jnp.float32)
            place = local + which * lines + u
            packed_ref[place : place + 1, :] = values
    atoms = atoms_ref[...]
    vectors = vectors_of(kinds_ref[0:1, :], readout_ref[...])
    energy, slope = layer(atoms, weights_ref[...], bias_ref[...], vectors)
    group_hot = hot(member_ref[0:1, :], GROUP_LOCAL)
    turned[...] = atoms.T
    for i in range(FEATURES):
        masked[SUB * i : SUB * i + SUB, :] = turned[i : i + 1, :] * group_hot
    grads = dot3(masked[...], slope)
    energies = jnp.sum(dot3(group_hot, energy), axis=1, keepdims=True)
    energies = jnp.broadcast_to(energies, (GROUP_LOCAL, FEATURES))
    blocks, _, wide = out_ref.shape
    per = FEATURES // blocks
    for j in range(blocks):
        for f in range(per):
            i = j * per + f
            out_ref[j, :, f * FEATURES : (f + 1) * FEATURES] = grads[SUB * i : SUB * i + SUB]
        out_ref[j, :, wide - FEATURES :] = energies


def first_terms(atoms, kinds, member, weights, bias, readout, cols, width):
    local = atoms.shape[1]
    return pl.pallas_call(
        first_kernel,
        grid=(1,),
        out_shape=(f32(cols, GROUP_LOCAL, width + FEATURES), f32(local + SUB, FEATURES)),
        in_specs=[
            pl.BlockSpec((None, local, FEATURES), lambda n: (0, 0, 0)),
            pl.BlockSpec((None, local, FEATURES), lambda n: (1, 0, 0)),
        ]
        + [whole()] * 5,
        out_specs=(whole(), whole()),
        scratch_shapes=[pltpu.VMEM((FEATURES, local), jnp.float32), pltpu.VMEM((SUB * FEATURES, local), jnp.float32)],
        compiler_params=params(63.9),
        name="first_terms",
    )(atoms, atoms, kinds, member, weights, bias, readout)


def prepare_kernel(col_ref, gathered_ref, readout_ref, atoms_ref, vectors_ref, masked_ref, turned):
    blocks = gathered_ref.shape[0]
    local = vectors_ref.shape[0] // blocks
    lines = local // FEATURES
    high_rows = (masked_ref.shape[0] - 2 * SUB) // 2
    count = high_rows // GROUP_LOCAL
    first = pl.multiple_of(col_ref[0] * count, SUB)
    for block in range(blocks):

        def row(start):
            parts = [gathered_ref[block, start + u : start + u + 1, :] for u in range(lines)]
            return jnp.concatenate(parts, axis=1).astype(jnp.int32)

        here = slice(block * local, (block + 1) * local)
        vectors_ref[here, :] = vectors_of(row(local), readout_ref[...])
        group_hot = hot(row(local + lines), GROUP_LOCAL)
        atoms = gathered_ref[block, :local, :]
        high, low = split(atoms)
        atoms_ref[here, :FEATURES] = high
        atoms_ref[here, FEATURES:] = low
        turned[block] = atoms.T
        part = turned[block, pl.ds(first, count), :]
        high, low = split(jnp.concatenate([part[f : f + 1, :] * group_hot for f in range(count)], axis=0))
        masked_ref[:high_rows, here] = high
        masked_ref[high_rows : 2 * high_rows, here] = low
        pair = jnp.concatenate([group_hot, jnp.zeros_like(group_hot)], axis=0)
        masked_ref[2 * high_rows :, here] = pair.astype(jnp.bfloat16)


def bf16(*shape):
    return jax.ShapeDtypeStruct(shape, jnp.bfloat16)


def prepare(gathered, readout, col_index, local, count):
    cols, tall, _ = gathered.shape
    lines = 2 * GROUP_LOCAL * (count + 1)
    parts = 4
    each = cols // parts
    return pl.pallas_call(
        prepare_kernel,
        grid=(parts,),
        out_shape=(bf16(cols * local, 2 * FEATURES), f32(cols * local, FEATURES), bf16(lines, cols * local)),
        in_specs=[scalar(), pl.BlockSpec((each, tall, FEATURES), lambda n: (n, 0, 0)), whole()],
        out_specs=(
            pl.BlockSpec((each * local, 2 * FEATURES), lambda n: (n, 0)),
            pl.BlockSpec((each * local, FEATURES), lambda n: (n, 0)),
            pl.BlockSpec((lines, each * local), lambda n: (0, n)),
        ),
        scratch_shapes=[pltpu.VMEM((each, FEATURES, local), jnp.float32)],
        compiler_params=params(63),
        name="prepare_terms",
    )(col_index, gathered, readout)


def later_kernel(atoms_ref, vectors_ref, masked_ref, weights_ref, bias_ref, out_ref, acc):
    step = pl.program_id(0)
    rows = masked_ref.shape[0] - 2 * SUB
    w_high, w_low = split(weights_ref[...])
    table = jnp.concatenate(
        [jnp.concatenate([w_high, w_low], axis=1), jnp.concatenate([w_high, jnp.zeros_like(w_low)], axis=1)], axis=0
    )
    preact = jnp.dot(atoms_ref[...], table, preferred_element_type=jnp.float32)
    hidden = jnp.tanh(preact[:, :FEATURES] + preact[:, FEATURES:] + bias_ref[...])
    vectors = vectors_ref[...]
    slope = jnp.concatenate(split((1.0 - hidden * hidden) * vectors), axis=1)
    energy = jnp.concatenate(split(hidden * vectors), axis=1)
    grads = jnp.dot(masked_ref[:rows, :], slope, preferred_element_type=jnp.float32)
    energies = jnp.dot(masked_ref[rows:, :], energy, preferred_element_type=jnp.float32)

    @pl.when(step == 0)
    def _():
        acc[:rows, :] = grads
        acc[rows:, :] = energies

    @pl.when(step > 0)
    def _():
        acc[:rows, :] += grads
        acc[rows:, :] += energies

    @pl.when(step == pl.num_programs(0) - 1)
    def _():
        both = acc[:, :FEATURES] + acc[:, FEATURES:]
        high_rows = rows // 2
        grads = both[:high_rows] + both[high_rows:rows]
        for f in range(high_rows // SUB):
            out_ref[:, f * FEATURES : (f + 1) * FEATURES] = grads[SUB * f : SUB * f + SUB]
        total_energy = jnp.sum(both[rows : rows + SUB], axis=1, keepdims=True)
        out_ref[:, high_rows // SUB * FEATURES :] = jnp.broadcast_to(total_energy, (GROUP_LOCAL, FEATURES))


def later_terms(terms, weights, bias):
    atoms, vectors, masked = terms
    parts = 4
    lines, count = masked.shape
    width = (lines // (2 * GROUP_LOCAL) - 1) * FEATURES
    each = count // parts
    return pl.pallas_call(
        later_kernel,
        grid=(parts,),
        out_shape=f32(GROUP_LOCAL, width + FEATURES),
        in_specs=[
            pl.BlockSpec((each, 2 * FEATURES), lambda n: (n, 0)),
            pl.BlockSpec((each, FEATURES), lambda n: (n, 0)),
            pl.BlockSpec((lines, each), lambda n: (0, n)),
            whole(),
            whole(),
        ],
        out_specs=whole(),
        scratch_shapes=[pltpu.VMEM((lines, 2 * FEATURES), jnp.float32)],
        compiler_params=params(63),
        name="later_terms",
    )(atoms, vectors, masked, weights, bias)


def downdate_kernel(scale, fresh, cov_ref, rows_ref, *rest):
    out_ref, table = rest[-2:]
    groups = table.shape[0] // 3

    @pl.when(pl.program_id(0) == 0)
    def _():
        if fresh:
            right = dot3(rest[0][...], rest[1][...]) * (1.0 / forget_rate)
        else:
            right = rest[0][...] * (1.0 / forget_rate**2)
        high, low = split(right)
        table[:groups, :] = high
        table[groups : 2 * groups, :] = high
        table[2 * groups :, :] = low

    left = rows_ref[:, :GROUP_LOCAL, :].reshape(groups, rows_ref.shape[2]).T
    high, low = split(left)
    change = jnp.dot(jnp.concatenate([high, low], axis=1), table[: 2 * groups, :], preferred_element_type=jnp.float32)
    change = change + jnp.dot(high, table[2 * groups :, :], preferred_element_type=jnp.float32)
    cov = cov_ref[...]
    out_ref[...] = (cov * scale if scale != 1.0 else cov) - change


def downdate(cov, gathered_rows, right, scale):
    rows, width = cov.shape
    part = 256
    cols, tall, _ = gathered_rows.shape
    return pl.pallas_call(
        functools.partial(downdate_kernel, scale, len(right) == 2),
        grid=(rows // part,),
        out_shape=f32(rows, width),
        in_specs=[
            pl.BlockSpec((part, width), lambda n: (n, 0)),
            pl.BlockSpec((cols, tall, part), lambda n: (0, 0, n)),
        ]
        + [whole()] * len(right),
        out_specs=pl.BlockSpec((part, width), lambda n: (n, 0)),
        scratch_shapes=[pltpu.VMEM((3 * GROUP_LOCAL * cols, width), jnp.bfloat16)],
        compiler_params=params(60.1),
        name="downdate",
    )(cov, gathered_rows, *right)


def pack_kernel(parts_ref, gains_ref, out_ref):
    width = gains_ref.shape[1]
    part = total(parts_ref[i] for i in range(parts_ref.shape[0]))
    for copy in range(out_ref.shape[0]):
        out_ref[copy, :, :width] = gains_ref[...]
        out_ref[copy, :, width:] = part


def pack(parts, gains, copies):
    sub, width = gains.shape
    return pl.pallas_call(
        pack_kernel,
        out_shape=f32(copies, sub, width + parts.shape[2]),
        in_specs=[whole(), whole()],
        out_specs=whole(),
        compiler_params=params(8),
        name="pack_gains",
    )(parts, gains)


def update_kernel(order, side_ref, own_ref, other_ref, energy_ref, targets_ref, inverse_ref, gains_ref, change_ref, both):
    n = targets_ref.shape[0]
    width = own_ref.shape[2] - n
    half = own_ref.shape[0]
    side = side_ref[0]
    both[pl.ds(side * half, half)] = own_ref[...]
    both[pl.ds((1 - side) * half, half)] = other_ref[...]
    places = [order.index(t) for t in range(n // SUB)]
    curvature = jnp.concatenate([both[p, :, width:] for p in places], axis=0)
    row = lax.broadcasted_iota(jnp.int32, (n, n), 0)
    col = lax.broadcasted_iota(jnp.int32, (n, n), 1)
    innovation = 0.5 * (curvature + curvature.T) + jnp.where(row == col, forget_rate, 0.0)
    tiles = sweep_inverse([innovation[SUB * i : SUB * i + SUB] for i in range(n // SUB)])
    weighted = []
    for i, x in enumerate(tiles):
        here = slice(SUB * i, SUB * i + SUB)
        inverse_ref[here, :] = x
        weighted.append(x * (targets_ref[here, :] - energy_ref[here, :]))
    coefficient = jnp.broadcast_to(jnp.sum(total(weighted), axis=0, keepdims=True), (SUB, n))
    gains = jnp.concatenate([both[p, :, :width] for p in places], axis=0)
    gains_ref[...] = gains
    moved = dot3(coefficient, gains)
    sub = lax.broadcasted_iota(jnp.int32, (SUB, FEATURES), 0)
    change = moved[:, :FEATURES]
    for r in range(1, width // FEATURES):
        change = jnp.where(sub == r, moved[:, r * FEATURES : (r + 1) * FEATURES], change)
    for j in range(change_ref.shape[0]):
        change_ref[j] = change


def solve_update(side, own, other, stacked, targets, copies, order):
    n = targets.shape[0]
    half, sub, wide = own.shape
    last = stacked.shape[1] // FEATURES - 1
    return pl.pallas_call(
        functools.partial(update_kernel, order),
        grid=(1,),
        out_shape=(f32(n, n), f32(n, wide - n), f32(copies, SUB, FEATURES)),
        in_specs=[scalar(), whole(), whole(), pl.BlockSpec((n, FEATURES), lambda i: (0, last)), whole()],
        out_specs=(whole(), whole(), whole()),
        scratch_shapes=[pltpu.VMEM((2 * half, sub, wide), jnp.float32)],
        compiler_params=params(8),
        name="inverse_and_change",
    )(side, own, other, stacked, targets)


def exchange(chunks, axis):
    return lax.all_to_all(chunks, axis, 0, 0, tiled=True)


def spread(x, axis):
    return exchange(jnp.broadcast_to(x[None], (lax.axis_size(axis),) + x.shape), axis)


def gather_pair(copies):
    count = copies.shape[0]
    lanes = [[core + 2 * z for z in range(count)] for core in range(2)]
    own = lax.all_to_all(copies, "grp", 0, 0, tiled=True, axis_index_groups=lanes)
    other = lax.ppermute(own, "grp", [(i, i ^ 1) for i in range(2 * count)])
    return own, other


def far_row(j, side):
    return (j // side + side // 2) % side * side + (j % side + side // 2) % side


def swap(x, chunk_of_row):
    size = len(chunk_of_row)
    pairs = [(i * size + chunk_of_row[a], a * size + i) for i in range(size) for a in range(size)]
    return lax.ppermute(x, ("grp", "atm"), pairs)


def gather_rows(own):
    twice = jnp.concatenate([own, own], axis=0)
    return lax.all_gather(twice, "atm", axis=0, tiled=False)


def together(*values):
    return lax.optimization_barrier(values)


def body(atoms, kinds, member, targets, weights, bias, readout, covariance):
    rows, cols = lax.axis_size("grp"), lax.axis_size("atm")
    chips = rows // 2
    col_index = lax.axis_index("atm").reshape(1)
    side = (lax.axis_index("grp") % 2).reshape(1)
    local = atoms.shape[1]
    groups = GROUP_LOCAL * rows
    width = covariance.shape[1]
    bias = bias.reshape(1, FEATURES)
    ordered = jnp.broadcast_to(targets[:, :, None], (STEPS, groups, FEATURES))
    chunk_of_row = [far_row(a, math.isqrt(rows)) for a in range(rows)]
    order = [chunk_of_row[2 * z + core] for core in range(2) for z in range(chips)]
    current = weights
    row_gains = []
    for step in range(STEPS):
        if step == 0:
            chunks, packed = first_terms(atoms, kinds, member, current, bias, readout, cols, width)
            gathered = lax.all_gather(packed, "atm", axis=0, tiled=False)
            chunk = exchange(chunks, "atm").sum(axis=0)
        else:
            chunk = later_terms(later, current, bias)
        stacked = lax.all_gather(chunk, "grp", axis=0, tiled=True)
        jac = stacked[:, :width]
        terms = dot(jac, covariance, ((1,), (1,)), three)
        if step:
            moved = dot(jac, scaled, ((1,), (1,)), three)
            gains = row_gains[0][:, :GROUP_LOCAL].reshape(groups, width)
            terms = (terms - dot(moved, gains, ((1,), (0,)), three)) / forget_rate
        own = exchange(terms.reshape(cols, groups // cols, width), "atm").sum(axis=0)
        if step == 0:
            own, gathered = together(own, gathered)
        row_gains.append(gather_rows(own))
        other = swap(own, chunk_of_row)
        if step == 0:
            later = prepare(gathered, readout, col_index, local, width // FEATURES)
            other, ordered, *later = together(other, ordered, *later)
        else:
            base = downdate(covariance, row_gains[0], (scaled,), 1.0 / forget_rate**2)
            other, base = together(other, base)
        part = spread(dot(other, jac, ((1,), (1,)), precise), "atm")
        got_own, got_other = gather_pair(pack(part, other, chips))
        inverse, col_gains, change = solve_update(
            side, got_own, got_other, stacked, ordered[step], cols, order
        )
        if step == STEPS - 1:
            change, row_gains[1] = together(change, row_gains[1])
        change = exchange(change, "atm")
        current = current + change.reshape(FEATURES, FEATURES)
        if step == 0:
            scaled = dot(inverse, col_gains, ((1,), (0,)), precise)
    covar = downdate(base, row_gains[1], (inverse, col_gains), 1.0)
    return (covar, current)


def solution(mesh):
    return jax.shard_map(
        body,
        mesh=mesh,
        in_specs=(
            P(None, ("grp", "atm"), None),
            P(None, ("grp", "atm")),
            P(None, ("grp", "atm")),
            P(),
            P(),
            P(),
            P(),
            P("grp", "atm"),
        ),
        out_specs=(P("grp", "atm"), P()),
        check_vma=False,
    )
```

```python
import functools
import math

import jax
import jax.numpy as jnp
from jax import lax
from jax.experimental import pallas as pl
from jax.experimental.pallas import tpu as pltpu
from jax.sharding import PartitionSpec as P

FEATURES = 128
GROUP_LOCAL = 8
STEPS = 2
SUB = 8

forget_rate = 0.98
precise = lax.Precision.HIGHEST
three = lax.Precision.HIGH
MIB = 1024 * 1024


def dot(a, b, contract, precision):
    return lax.dot_general(
        a, b, ((contract[0], contract[1]), ((), ())), precision=precision, preferred_element_type=jnp.float32
    )


def block_inverse(p):
    m = len(p)
    if m == 1:
        return [[1.0 / p[0][0]]]
    if m == 2:
        a, b, d = p[0][0], p[0][1], p[1][1]
        r = 1.0 / (a * d - b * b)
        return [[d * r, -b * r], [-b * r, a * r]]
    h = m // 2
    top = [[p[i][j] for j in range(h)] for i in range(h)]
    side = [[p[i][h + j] for j in range(h)] for i in range(h)]
    ti = block_inverse(top)
    ts = [[sum(ti[i][k] * side[k][j] for k in range(h)) for j in range(h)] for i in range(h)]
    schur = [[None] * h for _ in range(h)]
    for i in range(h):
        for j in range(i, h):
            schur[i][j] = p[h + i][h + j] - sum(side[k][i] * ts[k][j] for k in range(h))
            schur[j][i] = schur[i][j]
    si = block_inverse(schur)
    tss = [[sum(ts[i][k] * si[k][j] for k in range(h)) for j in range(h)] for i in range(h)]
    out = [[None] * m for _ in range(m)]
    for i in range(h):
        for j in range(h):
            out[i][h + j] = -tss[i][j]
            out[h + j][i] = -tss[i][j]
            out[h + i][h + j] = si[i][j]
            if j >= i:
                out[i][j] = ti[i][j] + sum(tss[i][k] * ts[j][k] for k in range(h))
                out[j][i] = out[i][j]
    return out


def total(values):
    values = list(values)
    while len(values) > 1:
        values = [values[i] + values[i + 1] if i + 1 < len(values) else values[i] for i in range(0, len(values), 2)]
    return values[0]


def sweep_inverse(tiles):
    n = tiles[0].shape[1]
    full = (SUB, n)
    lane = lax.broadcasted_iota(jnp.int32, (1, n), 1)
    sub = lax.broadcasted_iota(jnp.int32, (SUB, 1), 0)
    for t in range(n // SUB):
        k = t * SUB
        inside = (lane >= k) & (lane < k + SUB)
        rows = [tiles[t][u : u + 1, :] for u in range(SUB)]
        cols = [[jnp.broadcast_to(x[:, k + u : k + u + 1], full) for u in range(SUB)] for x in tiles]
        piv = [[cols[t][v][u : u + 1, :] for v in range(SUB)] for u in range(SUB)]
        inv = block_inverse(piv)
        rows = [jnp.where(inside, (lane == k + u).astype(jnp.float32), rows[u]) for u in range(SUB)]
        w = [total(inv[u][v] * rows[v] for v in range(SUB)) for u in range(SUB)]
        new = []
        for i, x in enumerate(tiles):
            if i == t:
                y = jnp.broadcast_to(w[0], full)
                for u in range(1, SUB):
                    y = jnp.where(sub == u, w[u], y)
            else:
                y = jnp.where(inside, 0.0, x) - total(cols[i][u] * w[u] for u in range(SUB))
            new.append(y)
        tiles = new
    return tiles


def split(x):
    high = x.astype(jnp.bfloat16)
    return high, (x - high.astype(jnp.float32)).astype(jnp.bfloat16)


def dot3(a, b, contract=((1,), (0,))):
    a_high, a_low = split(a)
    b_high, b_low = split(b)

    def one(x, y):
        return lax.dot_general(x, y, (contract, ((), ())), preferred_element_type=jnp.float32)

    return one(a_high, b_high) + (one(a_high, b_low) + one(a_low, b_high))


def exact(a, b, contract=((1,), (0,))):
    return lax.dot_general(a, b, (contract, ((), ())), precision=precise, preferred_element_type=jnp.float32)


def whole():
    return pl.BlockSpec(memory_space=pltpu.VMEM)


def scalar():
    return pl.BlockSpec(memory_space=pltpu.SMEM)


def params(mib):
    return pltpu.CompilerParams(vmem_limit_bytes=int(mib * MIB))


def f32(*shape):
    return jax.ShapeDtypeStruct(shape, jnp.float32)


def hot(values, count):
    return (lax.broadcasted_iota(jnp.int32, (count, values.shape[1]), 0) == values).astype(jnp.float32)


def vectors_of(kinds, readout):
    extra = 2 * SUB - readout.shape[0]
    table = jnp.concatenate([readout, jnp.zeros((extra, readout.shape[1]), jnp.float32)], axis=0)
    which = hot(kinds, 2 * SUB).astype(jnp.bfloat16)
    out = 0.0
    for _ in range(3):
        part = table.astype(jnp.bfloat16)
        table = table - part.astype(jnp.float32)
        out = out + lax.dot_general(which, part, (((0,), (0,)), ((), ())), preferred_element_type=jnp.float32)
    return out


def layer(atoms, weights, bias, vectors):
    hidden = jnp.tanh(dot3(atoms, weights) + bias)
    return hidden * vectors, (1.0 - hidden * hidden) * vectors


def first_kernel(
    atoms_ref, next_ref, kinds_ref, member_ref, weights_ref, bias_ref, readout_ref, out_ref, packed_ref, turned, masked
):
    local = next_ref.shape[0]
    lines = local // FEATURES
    packed_ref[:local, :] = next_ref[...]
    packed_ref[local:, :] = jnp.zeros((packed_ref.shape[0] - local, FEATURES), jnp.float32)
    for which, ref in enumerate((kinds_ref, member_ref)):
        for u in range(lines):
            values = ref[1:2, u * FEATURES : (u + 1) * FEATURES].astype(jnp.float32)
            place = local + which * lines + u
            packed_ref[place : place + 1, :] = values
    atoms = atoms_ref[...]
    vectors = vectors_of(kinds_ref[0:1, :], readout_ref[...])
    energy, slope = layer(atoms, weights_ref[...], bias_ref[...], vectors)
    group_hot = hot(member_ref[0:1, :], GROUP_LOCAL)
    turned[...] = atoms.T
    for i in range(FEATURES):
        masked[SUB * i : SUB * i + SUB, :] = turned[i : i + 1, :] * group_hot
    grads = dot3(masked[...], slope)
    energies = jnp.sum(dot3(group_hot, energy), axis=1, keepdims=True)
    energies = jnp.broadcast_to(energies, (GROUP_LOCAL, FEATURES))
    blocks, _, wide = out_ref.shape
    per = FEATURES // blocks
    for j in range(blocks):
        for f in range(per):
            i = j * per + f
            out_ref[j, :, f * FEATURES : (f + 1) * FEATURES] = grads[SUB * i : SUB * i + SUB]
        out_ref[j, :, wide - FEATURES :] = energies


def first_terms(atoms, kinds, member, weights, bias, readout, cols, width):
    local = atoms.shape[1]
    return pl.pallas_call(
        first_kernel,
        grid=(1,),
        out_shape=(f32(cols, GROUP_LOCAL, width + FEATURES), f32(local + SUB, FEATURES)),
        in_specs=[
            pl.BlockSpec((None, local, FEATURES), lambda n: (0, 0, 0)),
            pl.BlockSpec((None, local, FEATURES), lambda n: (1, 0, 0)),
        ]
        + [whole()] * 5,
        out_specs=(whole(), whole()),
        scratch_shapes=[pltpu.VMEM((FEATURES, local), jnp.float32), pltpu.VMEM((SUB * FEATURES, local), jnp.float32)],
        compiler_params=params(63.9),
        name="first_terms",
    )(atoms, atoms, kinds, member, weights, bias, readout)


def prepare_kernel(col_ref, gathered_ref, readout_ref, atoms_ref, vectors_ref, masked_ref, turned):
    blocks = gathered_ref.shape[0]
    local = vectors_ref.shape[0] // blocks
    lines = local // FEATURES
    high_rows = (masked_ref.shape[0] - 2 * SUB) // 2
    count = high_rows // GROUP_LOCAL
    first = pl.multiple_of(col_ref[0] * count, SUB)
    for block in range(blocks):

        def row(start):
            parts = [gathered_ref[block, start + u : start + u + 1, :] for u in range(lines)]
            return jnp.concatenate(parts, axis=1).astype(jnp.int32)

        here = slice(block * local, (block + 1) * local)
        vectors_ref[here, :] = vectors_of(row(local), readout_ref[...])
        group_hot = hot(row(local + lines), GROUP_LOCAL)
        atoms = gathered_ref[block, :local, :]
        high, low = split(atoms)
        atoms_ref[here, :FEATURES] = high
        atoms_ref[here, FEATURES:] = low
        turned[block] = atoms.T
        part = turned[block, pl.ds(first, count), :]
        high, low = split(jnp.concatenate([part[f : f + 1, :] * group_hot for f in range(count)], axis=0))
        masked_ref[:high_rows, here] = high
        masked_ref[high_rows : 2 * high_rows, here] = low
        pair = jnp.concatenate([group_hot, jnp.zeros_like(group_hot)], axis=0)
        masked_ref[2 * high_rows :, here] = pair.astype(jnp.bfloat16)


def bf16(*shape):
    return jax.ShapeDtypeStruct(shape, jnp.bfloat16)


def prepare(gathered, readout, col_index, local, count):
    cols, tall, _ = gathered.shape
    lines = 2 * GROUP_LOCAL * (count + 1)
    parts = 4
    each = cols // parts
    return pl.pallas_call(
        prepare_kernel,
        grid=(parts,),
        out_shape=(bf16(cols * local, 2 * FEATURES), f32(cols * local, FEATURES), bf16(lines, cols * local)),
        in_specs=[scalar(), pl.BlockSpec((each, tall, FEATURES), lambda n: (n, 0, 0)), whole()],
        out_specs=(
            pl.BlockSpec((each * local, 2 * FEATURES), lambda n: (n, 0)),
            pl.BlockSpec((each * local, FEATURES), lambda n: (n, 0)),
            pl.BlockSpec((lines, each * local), lambda n: (0, n)),
        ),
        scratch_shapes=[pltpu.VMEM((each, FEATURES, local), jnp.float32)],
        compiler_params=params(63),
        name="prepare_terms",
    )(col_index, gathered, readout)


def later_kernel(atoms_ref, vectors_ref, masked_ref, weights_ref, change_ref, bias_ref, out_ref, acc):
    step = pl.program_id(0)
    rows = masked_ref.shape[0] - 2 * SUB
    w_high, w_low = split(weights_ref[...] + change_ref[...].reshape(FEATURES, FEATURES))
    table = jnp.concatenate(
        [jnp.concatenate([w_high, w_low], axis=1), jnp.concatenate([w_high, jnp.zeros_like(w_low)], axis=1)], axis=0
    )
    preact = jnp.dot(atoms_ref[...], table, preferred_element_type=jnp.float32)
    hidden = jnp.tanh(preact[:, :FEATURES] + preact[:, FEATURES:] + bias_ref[...])
    vectors = vectors_ref[...]
    slope = jnp.concatenate(split((1.0 - hidden * hidden) * vectors), axis=1)
    energy = jnp.concatenate(split(hidden * vectors), axis=1)
    grads = jnp.dot(masked_ref[:rows, :], slope, preferred_element_type=jnp.float32)
    energies = jnp.dot(masked_ref[rows:, :], energy, preferred_element_type=jnp.float32)

    @pl.when(step == 0)
    def _():
        acc[:rows, :] = grads
        acc[rows:, :] = energies

    @pl.when(step > 0)
    def _():
        acc[:rows, :] += grads
        acc[rows:, :] += energies

    @pl.when(step == pl.num_programs(0) - 1)
    def _():
        both = acc[:, :FEATURES] + acc[:, FEATURES:]
        high_rows = rows // 2
        grads = both[:high_rows] + both[high_rows:rows]
        for f in range(high_rows // SUB):
            out_ref[:, f * FEATURES : (f + 1) * FEATURES] = grads[SUB * f : SUB * f + SUB]
        total_energy = jnp.sum(both[rows : rows + SUB], axis=1, keepdims=True)
        out_ref[:, high_rows // SUB * FEATURES :] = jnp.broadcast_to(total_energy, (GROUP_LOCAL, FEATURES))


def later_terms(terms, weights, change, bias):
    atoms, vectors, masked = terms
    parts = 4
    lines, count = masked.shape
    width = (lines // (2 * GROUP_LOCAL) - 1) * FEATURES
    each = count // parts
    return pl.pallas_call(
        later_kernel,
        grid=(parts,),
        out_shape=f32(GROUP_LOCAL, width + FEATURES),
        in_specs=[
            pl.BlockSpec((each, 2 * FEATURES), lambda n: (n, 0)),
            pl.BlockSpec((each, FEATURES), lambda n: (n, 0)),
            pl.BlockSpec((lines, each), lambda n: (0, n)),
            whole(),
            whole(),
            whole(),
        ],
        out_specs=whole(),
        scratch_shapes=[pltpu.VMEM((lines, 2 * FEATURES), jnp.float32)],
        compiler_params=params(63),
        name="later_terms",
    )(atoms, vectors, masked, weights, change, bias)


def downdate_kernel(scale, fresh, cov_ref, rows_ref, *rest):
    out_ref, table = rest[-2:]
    groups = table.shape[0] // 3

    @pl.when(pl.program_id(0) == 0)
    def _():
        if fresh:
            right = dot3(rest[0][...], rest[1][...]) * (1.0 / forget_rate)
        else:
            right = rest[0][...] * (1.0 / forget_rate**2)
        high, low = split(right)
        table[:groups, :] = high
        table[groups : 2 * groups, :] = high
        table[2 * groups :, :] = low

    left = rows_ref[:, :GROUP_LOCAL, :].reshape(groups, rows_ref.shape[2]).T
    high, low = split(left)
    change = jnp.dot(jnp.concatenate([high, low], axis=1), table[: 2 * groups, :], preferred_element_type=jnp.float32)
    change = change + jnp.dot(high, table[2 * groups :, :], preferred_element_type=jnp.float32)
    cov = cov_ref[...]
    out_ref[...] = (cov * scale if scale != 1.0 else cov) - change


def downdate(cov, gathered_rows, right, scale):
    rows, width = cov.shape
    part = 256
    cols, tall, _ = gathered_rows.shape
    return pl.pallas_call(
        functools.partial(downdate_kernel, scale, len(right) == 2),
        grid=(rows // part,),
        out_shape=f32(rows, width),
        in_specs=[
            pl.BlockSpec((part, width), lambda n: (n, 0)),
            pl.BlockSpec((cols, tall, part), lambda n: (0, 0, n)),
        ]
        + [whole()] * len(right),
        out_specs=pl.BlockSpec((part, width), lambda n: (n, 0)),
        scratch_shapes=[pltpu.VMEM((3 * GROUP_LOCAL * cols, width), jnp.bfloat16)],
        compiler_params=params(60.1),
        name="downdate",
    )(cov, gathered_rows, *right)


def pack_kernel(parts_ref, gains_ref, out_ref):
    width = gains_ref.shape[1]
    part = total(parts_ref[i] for i in range(parts_ref.shape[0]))
    for copy in range(out_ref.shape[0]):
        out_ref[copy, :, :width] = gains_ref[...]
        out_ref[copy, :, width:] = part


def pack(parts, gains, copies):
    sub, width = gains.shape
    return pl.pallas_call(
        pack_kernel,
        out_shape=f32(copies, sub, width + parts.shape[2]),
        in_specs=[whole(), whole()],
        out_specs=whole(),
        compiler_params=params(8),
        name="pack_gains",
    )(parts, gains)


def update_kernel(order, side_ref, own_ref, other_ref, energy_ref, targets_ref, inverse_ref, gains_ref, change_ref, both):
    n = targets_ref.shape[0]
    width = own_ref.shape[2] - n
    half = own_ref.shape[0]
    side = side_ref[0]
    both[pl.ds(side * half, half)] = own_ref[...]
    both[pl.ds((1 - side) * half, half)] = other_ref[...]
    places = [order.index(t) for t in range(n // SUB)]
    curvature = jnp.concatenate([both[p, :, width:] for p in places], axis=0)
    row = lax.broadcasted_iota(jnp.int32, (n, n), 0)
    col = lax.broadcasted_iota(jnp.int32, (n, n), 1)
    innovation = 0.5 * (curvature + curvature.T) + jnp.where(row == col, forget_rate, 0.0)
    tiles = sweep_inverse([innovation[SUB * i : SUB * i + SUB] for i in range(n // SUB)])
    weighted = []
    for i, x in enumerate(tiles):
        here = slice(SUB * i, SUB * i + SUB)
        inverse_ref[here, :] = x
        weighted.append(x * (targets_ref[here, :] - energy_ref[here, :]))
    coefficient = jnp.broadcast_to(jnp.sum(total(weighted), axis=0, keepdims=True), (SUB, n))
    gains = jnp.concatenate([both[p, :, :width] for p in places], axis=0)
    gains_ref[...] = gains
    moved = dot3(coefficient, gains)
    sub = lax.broadcasted_iota(jnp.int32, (SUB, FEATURES), 0)
    change = moved[:, :FEATURES]
    for r in range(1, width // FEATURES):
        change = jnp.where(sub == r, moved[:, r * FEATURES : (r + 1) * FEATURES], change)
    for j in range(change_ref.shape[0]):
        change_ref[j] = change


def solve_update(side, own, other, stacked, targets, copies, order):
    n = targets.shape[0]
    half, sub, wide = own.shape
    last = stacked.shape[1] // FEATURES - 1
    return pl.pallas_call(
        functools.partial(update_kernel, order),
        grid=(1,),
        out_shape=(f32(n, n), f32(n, wide - n), f32(copies, SUB, FEATURES)),
        in_specs=[scalar(), whole(), whole(), pl.BlockSpec((n, FEATURES), lambda i: (0, last)), whole()],
        out_specs=(whole(), whole(), whole()),
        scratch_shapes=[pltpu.VMEM((2 * half, sub, wide), jnp.float32)],
        compiler_params=params(8),
        name="inverse_and_change",
    )(side, own, other, stacked, targets)


def exchange(chunks, axis):
    return lax.all_to_all(chunks, axis, 0, 0, tiled=True)


def spread(x, axis):
    return exchange(jnp.broadcast_to(x[None], (lax.axis_size(axis),) + x.shape), axis)


def gather_pair(copies):
    count = copies.shape[0]
    lanes = [[core + 2 * z for z in range(count)] for core in range(2)]
    own = lax.all_to_all(copies, "grp", 0, 0, tiled=True, axis_index_groups=lanes)
    other = lax.ppermute(own, "grp", [(i, i ^ 1) for i in range(2 * count)])
    return own, other


def far_row(j, side):
    return (j // side + side // 2) % side * side + (j % side + side // 2) % side


def swap(x, chunk_of_row):
    size = len(chunk_of_row)
    pairs = [(i * size + chunk_of_row[a], a * size + i) for i in range(size) for a in range(size)]
    return lax.ppermute(x, ("grp", "atm"), pairs)


def gather_rows(own):
    twice = jnp.concatenate([own, own], axis=0)
    return lax.all_gather(twice, "atm", axis=0, tiled=False)


def together(*values):
    return lax.optimization_barrier(values)


def body(atoms, kinds, member, targets, weights, bias, readout, covariance):
    rows, cols = lax.axis_size("grp"), lax.axis_size("atm")
    chips = rows // 2
    col_index = lax.axis_index("atm").reshape(1)
    side = (lax.axis_index("grp") % 2).reshape(1)
    local = atoms.shape[1]
    groups = GROUP_LOCAL * rows
    width = covariance.shape[1]
    bias = bias.reshape(1, FEATURES)
    ordered = jnp.broadcast_to(targets[:, :, None], (STEPS, groups, FEATURES))
    chunk_of_row = [far_row(a, math.isqrt(rows)) for a in range(rows)]
    order = [chunk_of_row[2 * z + core] for core in range(2) for z in range(chips)]
    current = weights
    row_gains = []
    for step in range(STEPS):
        if step == 0:
            chunks, packed = first_terms(atoms, kinds, member, current, bias, readout, cols, width)
            gathered = lax.all_gather(packed, "atm", axis=0, tiled=False)
            chunk = exchange(chunks, "atm").sum(axis=0)
        else:
            chunk = later_terms(later, weights, change, bias)
        stacked = lax.all_gather(chunk, "grp", axis=0, tiled=True)
        jac = stacked[:, :width]
        terms = dot(jac, covariance, ((1,), (1,)), three)
        if step:
            moved = dot(jac, scaled, ((1,), (1,)), three)
            gains = row_gains[0][:, :GROUP_LOCAL].reshape(groups, width)
            terms = (terms - dot(moved, gains, ((1,), (0,)), three)) / forget_rate
        own = exchange(terms.reshape(cols, groups // cols, width), "atm").sum(axis=0)
        if step == 0:
            own, gathered = together(own, gathered)
        row_gains.append(gather_rows(own))
        other = swap(own, chunk_of_row)
        if step == 0:
            later = prepare(gathered, readout, col_index, local, width // FEATURES)
            other, ordered, *later = together(other, ordered, *later)
        else:
            base = downdate(covariance, row_gains[0], (scaled,), 1.0 / forget_rate**2)
            other, base = together(other, base)
        part = spread(dot(other, jac, ((1,), (1,)), precise), "atm")
        got_own, got_other = gather_pair(pack(part, other, chips))
        inverse, col_gains, change = solve_update(
            side, got_own, got_other, stacked, ordered[step], cols, order
        )
        if step == STEPS - 1:
            change, row_gains[1] = together(change, row_gains[1])
        change = exchange(change, "atm")
        current = current + change.reshape(FEATURES, FEATURES)
        if step == 0:
            scaled = dot(inverse, col_gains, ((1,), (0,)), precise)
    covar = downdate(base, row_gains[1], (inverse, col_gains), 1.0)
    return (covar, current)


def solution(mesh):
    return jax.shard_map(
        body,
        mesh=mesh,
        in_specs=(
            P(None, ("grp", "atm"), None),
            P(None, ("grp", "atm")),
            P(None, ("grp", "atm")),
            P(),
            P(),
            P(),
            P(),
            P("grp", "atm"),
        ),
        out_specs=(P("grp", "atm"), P()),
        check_vma=False,
    )
```
